32 devices in a mesh: grp: 2 (over x), ctx: 4 (over y, core), exp: 4 (over z).
Axes of the slice: x: 2, y: 2, z: 4, core: 2. Of those that a mesh axis runs over, the one named last changes fastest.
Arguments:
- hidden_in: bfloat16 [8, 1024, 2048], P(('grp', 'exp'), 'ctx'), may hold values from -6 to 6
- out_grad: bfloat16 [8, 1024, 2048], P(('grp', 'exp'), 'ctx'), may hold values from -6 to 6
- doc_lengths: int32 [8, 6], P(('grp', 'exp')), may hold values from 1 to 1019, as said below
- routes: int32 [8, 1024, 8], P(('grp', 'exp'), 'ctx'), may hold values from 0 to 15, all different within a row; in each aligned block of 256 rows (0 to 255, 256 to 511, ..., all dimensions but the last counted through in order) at most 160 rows name the same one
- attention_input_weight: bfloat16 [2048, 5120], P(('ctx', 'exp')), may hold values from -0.125 to 0.125
- attn_out_weight: bfloat16 [2048, 4096], P(('ctx', 'exp')), may hold values from -0.75 to 0.75
- norm_gains: bfloat16 [2048, 2], replicated, may hold values from 0.25 to 1.75
- head_gains: bfloat16 [128, 2], replicated, may hold values from 0.25 to 1.75
- router_weight: bfloat16 [2048, 16], replicated, may hold values from -0.06591797 to 0.06591797
- expert_in: bfloat16 [2048, 16, 2, 768], P('ctx', 'exp'), may hold values from -0.125 to 0.125
- expert_out: bfloat16 [2048, 16, 768], P('ctx', 'exp'), may hold values from -0.875 to 0.875
Outputs:
- output: bfloat16 [8, 1024, 2048], P(('grp', 'exp'), 'ctx')
- input_grad: bfloat16 [8, 1024, 2048], P(('grp', 'exp'), 'ctx')
- attn_in_grad: float32 [2048, 5120], P(('ctx', 'exp'))
- attn_out_grad: float32 [2048, 4096], P(('ctx', 'exp'))
- norm_gains_grad: float32 [2048, 2], replicated
- head_gains_grad: float32 [128, 2], replicated
- router_grad: float32 [2048, 16], replicated
- expert_in_grad: float32 [2048, 16, 2, 768], P('ctx', 'exp')
- expert_out_grad: float32 [2048, 16, 768], P('ctx', 'exp')
The draws below stay inside these ranges and needn't reach their ends.
Inputs may be any that keep to these rules, and one draw needn't show every extreme that they name: `doc_lengths`: each row lists the lengths of the 6 documents of one sequence in order; they sum to 1024. A token's 8 routes name different experts; among the tokens of one device (aligned blocks of 256 positions) no expert is named more than 160 times, a bound that some block reaches.
All inputs are finite; a program needn't handle non-finite values.
Results may differ from the reference program's by a relative error of at most 0.02.
Values may be sent and summed in bfloat16 or wider, within the bound.
A program may use at most 512 MiB of HBM per device.

```python
import math
import jax
import jax.numpy as jnp
import numpy as np
from jax import lax

MODEL_DIMENSION = 2048
QUERY_HEADS = 32
KEY_VALUE_HEADS = 4
HEAD_SIZE = 128
FF = 768
TOP = 8
EXPERTS = 16
NDOC = 6
LEN = 1024
ROWS = 256
SEQS = 8
CAP = 160
N_CTX = 4


def draw_doc_lengths(key, part):
    key = jax.random.fold_in(key, 11)
    pick_key, size_key = jax.random.split(key)
    longest = jax.random.randint(pick_key, (SEQS, 1), 0, NDOC)
    shorts = jax.random.randint(size_key, (SEQS, NDOC), 1, ROWS // NDOC + 1)
    first_row = jnp.arange(SEQS)[:, None] == 0
    shorts = jnp.where(first_row, 1, shorts)
    placed = jnp.arange(NDOC)[None, :] == longest
    others = jnp.sum(jnp.where(placed, 0, shorts), axis=1, keepdims=True)
    return jnp.where(placed, LEN - others, shorts).astype(jnp.int32)


def steps_of(stream_key, extent, shards, smallest, largest):
    def one(dim, shards_of):
        steps = jax.random.uniform(jax.random.fold_in(jax.random.fold_in(stream_key, 6), dim), (shards_of,), jnp.float32, smallest / len(shards), largest / len(shards))
        return jnp.repeat(jnp.exp(steps), extent[dim] // shards_of).reshape((-1,) + (1,) * (len(extent) - dim - 1))

    factor_of = one(*shards[0])
    for cut in shards[1:]:
        factor_of = factor_of * one(*cut)
    return factor_of


def deal_out(stream_key, own, number, rows, amount, top, reach, slope):
    order = jax.random.permutation(stream_key, amount)
    packed, ordinary = load_shares(amount, rows * top, reach, slope, True), load_shares(amount, rows * top, reach, slope, False)
    places = jnp.arange(amount)

    def named(sizes, rotation):
        used = int((sizes > 0).sum())
        fixed = max(1, used // 4)
        moved = fixed + (places - fixed + rotation * (used - fixed)) % max(1, amount - fixed)
        return jnp.zeros((amount,), jnp.int32).at[order[jnp.where(places < fixed, places, moved)]].set(jnp.asarray(sizes, jnp.int32))

    sizes = jnp.where(number % 4 == 0, named(packed, number // 4), named(ordinary, number - number // 4 - 1))
    mixed = jax.random.permutation(jax.random.fold_in(own, 3), amount)
    donor, sink = mixed[0:amount // 2 * 2:2], mixed[1:amount // 2 * 2:2]
    room = jnp.minimum(sizes[donor] - 1, reach - sizes[sink]) // 2
    room = jnp.where((donor == order[0]) | (sink == order[0]) | (sizes[sink] == 0), 0, jnp.maximum(room, 0))
    moved = jax.random.randint(jax.random.fold_in(own, 4), (amount // 2,), 0, 1 << 20) % (room + 1)
    sizes = sizes.at[donor].add(-moved).at[sink].add(moved)
    labels = jnp.searchsorted(jnp.cumsum(sizes), jnp.arange(rows * top), side="right").astype(jnp.int32)
    table = labels.reshape(top, rows).T
    table = table[jax.random.permutation(jax.random.fold_in(own, 1), rows)]
    rotation = jax.random.randint(jax.random.fold_in(own, 2), (rows, 1), 0, top)
    return jnp.take_along_axis(table, (jnp.arange(top)[None, :] + rotation) % top, axis=1)


def load_shares(number_of, total, most, lean, full):
    loads = [(1 << 20) // math.isqrt(grade ** lean) + 1 for grade in range(1, number_of + 1)]
    largest = most if full else min(most, max(-(-total // number_of), total * loads[0] // sum(loads)))
    least = 1 if total - largest >= number_of - 1 else 0
    given, surplus = [largest] + [least] * (number_of - 1), total - largest - least * (number_of - 1)
    while surplus > 0:
        candidates = [i for i in range(1, number_of) if given[i] < largest] or [i for i in range(1, number_of) if given[i] < most]
        pool, left = sum([loads[i] for i in candidates]), surplus
        for i in candidates:
            extra = min(most - given[i], max(1, left * loads[i] // pool), surplus)
            given[i] = given[i] + extra
            surplus = surplus - extra
    return np.array(given)


def scatter_about(key, extent, deviation, limit, pieces=(), held_as=jnp.bfloat16):
    values = jax.random.normal(key, extent, jnp.float32) * deviation
    if len(pieces) > 0:
        values = steps_of(key, extent, pieces, -0.22, 0.18) * values
    return jnp.clip(values, min=-limit, max=limit).astype(held_as)


def setup_inputs(seed: int = 0) -> dict:
    key_of = jax.random.split(jax.random.key(seed), 12)
    hidden_in = scatter_about(key_of[0], (SEQS, LEN, MODEL_DIMENSION), 1.0, 6.0, ((0, 8), (1, 4)))
    out_grad = scatter_about(key_of[1], (SEQS, LEN, MODEL_DIMENSION), 1.0, 6.0, ((0, 8), (1, 4)))
    doc_lengths = draw_doc_lengths(jax.random.fold_in(key_of[11], 71), 0)
    routes_keys = jax.random.split(jax.random.fold_in(key_of[3], 1), SEQS * LEN // ROWS)
    routes_turns = jax.random.permutation(jax.random.fold_in(key_of[3], 3), SEQS * LEN // ROWS)
    routes = jax.vmap(lambda own, number: deal_out(jax.random.fold_in(key_of[3], 2), own, number, ROWS, EXPERTS, TOP, CAP, 1))(routes_keys, routes_turns).reshape((SEQS, LEN, TOP))
    attention_input_weight = scatter_about(key_of[4], (MODEL_DIMENSION, (QUERY_HEADS + 2 * KEY_VALUE_HEADS) * HEAD_SIZE), MODEL_DIMENSION ** -0.5, 0.125, ((0, 16),))
    attn_out_weight = scatter_about(key_of[5], (MODEL_DIMENSION, QUERY_HEADS * HEAD_SIZE), (QUERY_HEADS * HEAD_SIZE // 64) ** -0.5, 0.75, ((0, 16),))
    norm_gains = jnp.clip(1.0 + 0.15 * jax.random.normal(key_of[6], (MODEL_DIMENSION, 2), jnp.float32), 0.25, 1.75).astype(jnp.bfloat16)
    head_gains = jnp.clip(1.0 + 0.15 * jax.random.normal(key_of[7], (HEAD_SIZE, 2), jnp.float32), 0.25, 1.75).astype(jnp.bfloat16)
    router_weight = scatter_about(key_of[8], (MODEL_DIMENSION, EXPERTS), 0.011, 0.06591797)
    expert_in = scatter_about(key_of[9], (MODEL_DIMENSION, EXPERTS, 2, FF), MODEL_DIMENSION ** -0.5, 0.125, ((0, 4), (1, 4)))
    expert_out = scatter_about(key_of[10], (MODEL_DIMENSION, EXPERTS, FF), (FF // 16) ** -0.5, 0.875, ((0, 4), (1, 4)))
    return {"hidden_in": hidden_in, "out_grad": out_grad, "doc_lengths": doc_lengths, "routes": routes, "attention_input_weight": attention_input_weight, "attn_out_weight": attn_out_weight, "norm_gains": norm_gains, "head_gains": head_gains, "router_weight": router_weight, "expert_in": expert_in, "expert_out": expert_out}


epsilon = 1e-06
rotary_base = 1000000.0
highest = lax.Precision.HIGHEST

@jax.custom_vjp
def low(v):
    return lax.optimization_barrier(v.astype(jnp.bfloat16)).astype(jnp.float32)

@jax.custom_vjp
def low_back(v):
    return v

def low_keep(v):
    return (low(v), None)

def low_pass(kept, grad):
    return (grad,)

def back_keep(v):
    return (v, None)

def back_low(kept, grad):
    return (low(grad),)
low.defvjp(low_keep, low_pass)
low_back.defvjp(back_keep, back_low)

def doc_tables(lengths, positions):
    doc_ends = jnp.cumsum(lengths).astype(jnp.int32)
    passed = positions[:, None] >= doc_ends[None, :]
    doc_index = lax.optimization_barrier(jnp.sum(passed.astype(jnp.int32), axis=1)).astype(jnp.int32)
    first_pos = lax.optimization_barrier(jnp.sum(jnp.where(passed, lengths[None, :], 0), axis=1)).astype(jnp.int32)
    return (doc_index, positions - first_pos)

def rotate(values, relative, sign):
    half_dim = values.shape[-1] // 2
    freqs = rotary_base ** (-2.0 * jnp.arange(half_dim, dtype=jnp.float32) / values.shape[-1])
    angles = relative.astype(jnp.float32)[:, None] * freqs[None, :]
    cosine = jnp.cos(angles)[:, None, :]
    sine = sign * jnp.sin(angles)[:, None, :]
    first = values[..., :half_dim]
    second = values[..., half_dim:]
    return jnp.concatenate([first * cosine - second * sine, second * cosine + first * sine], axis=-1)

def rms_norm(values, gain_vec):
    scaled = values * lax.rsqrt(lax.optimization_barrier(jnp.mean(values * values, axis=-1, keepdims=True)) + epsilon)
    return scaled * gain_vec

def attention(queries, key_head_rows, value_head_rows, doc_index):
    token_length = queries.shape[0]
    span = min(512, token_length)
    query_group_size = QUERY_HEADS // KEY_VALUE_HEADS
    keys_wide = jnp.repeat(key_head_rows, query_group_size, axis=1)
    values_wide = jnp.repeat(value_head_rows, query_group_size, axis=1)
    positions = jnp.arange(token_length, dtype=jnp.int32)
    score_scale = HEAD_SIZE ** (-0.5)

    def one_block(block_id):
        begin = (block_id * span).astype(jnp.int32)
        query_block = lax.dynamic_slice_in_dim(queries, begin, span, 0)
        query_pos = lax.dynamic_slice_in_dim(positions, begin, span, 0)
        query_doc = lax.dynamic_slice_in_dim(doc_index, begin, span, 0)
        raw_scores = jnp.einsum('qhd,khd->hqk', query_block, keys_wide, precision=highest)
        scores = low_back(raw_scores * score_scale)
        allowed = (positions[None, :] <= query_pos[:, None]) & (doc_index[None, :] == query_doc[:, None])
        scores = jnp.where(allowed[None], scores, -1e+30)
        weights = low(jax.nn.softmax(scores, axis=-1))
        return jnp.einsum('hqk,khd->qhd', weights, values_wide, precision=highest)
    blocks = lax.map(jax.checkpoint(one_block), jnp.arange(token_length // span, dtype=jnp.int32))
    return blocks.reshape(token_length, QUERY_HEADS * HEAD_SIZE)

def experts(sent, route, expert_in, expert_out):
    token_length = route.shape[0]
    flat_rows = token_length * TOP
    room = N_CTX * CAP
    padded = jnp.concatenate([sent.reshape(flat_rows, MODEL_DIMENSION), jnp.zeros((1, MODEL_DIMENSION), sent.dtype)], axis=0)
    flat_route = route.reshape(flat_rows)

    def one_expert(expert_id):
        picked = jnp.nonzero(flat_route == expert_id, size=room, fill_value=flat_rows)[0].astype(jnp.int32)
        inputs = padded[picked]
        weight_in = lax.dynamic_index_in_dim(expert_in, expert_id, 1, keepdims=False)
        weight_out = lax.dynamic_index_in_dim(expert_out, expert_id, 1, keepdims=False)
        gate_up = low_back(jnp.einsum('md,dkf->mkf', inputs, weight_in, precision=highest))
        active = low(jax.nn.silu(gate_up[:, 0]) * gate_up[:, 1])
        made = low_back(low(jnp.einsum('mf,df->md', active, weight_out, precision=highest)))
        return (picked, made)
    picked, made = lax.map(jax.checkpoint(one_expert), jnp.arange(EXPERTS, dtype=jnp.int32))
    gathered = jnp.zeros((flat_rows + 1, MODEL_DIMENSION), sent.dtype).at[picked.reshape(-1)].add(made.reshape(-1, MODEL_DIMENSION))
    return gathered[:flat_rows].reshape(token_length, TOP, MODEL_DIMENSION)

def layer(hidden, attn_in, attn_out, norm_gains, head_gains, router, expert_in, expert_out, lengths, route):
    token_length = hidden.shape[0]
    positions = jnp.arange(token_length, dtype=jnp.int32)
    doc_index, relative = doc_tables(lengths, positions)
    normed = low(rms_norm(hidden, norm_gains[:, 0]))
    joined_projection = low_back(jnp.dot(normed, attn_in, precision=highest))
    queries = joined_projection[:, :QUERY_HEADS * HEAD_SIZE].reshape(token_length, QUERY_HEADS, HEAD_SIZE)
    key_head_rows = joined_projection[:, QUERY_HEADS * HEAD_SIZE:(QUERY_HEADS + KEY_VALUE_HEADS) * HEAD_SIZE].reshape(token_length, KEY_VALUE_HEADS, HEAD_SIZE)
    value_head_rows = joined_projection[:, (QUERY_HEADS + KEY_VALUE_HEADS) * HEAD_SIZE:].reshape(token_length, KEY_VALUE_HEADS, HEAD_SIZE)
    queries = low(rotate(rms_norm(queries, head_gains[:, 0]), relative, 1.0))
    key_head_rows = low(rotate(rms_norm(key_head_rows, head_gains[:, 1]), relative, 1.0))
    value_head_rows = low(value_head_rows)
    attended = low(attention(queries, key_head_rows, value_head_rows, doc_index))
    branch = low_back(jnp.einsum('rc,dc->rd', attended, attn_out, precision=highest))
    middle = hidden + branch
    ffn_normed = low(rms_norm(middle, norm_gains[:, 1]))
    logits = jnp.dot(ffn_normed, router, precision=highest)
    probs = jax.nn.softmax(logits, axis=-1)
    selected = jnp.take_along_axis(probs, route, axis=1)
    gates = selected / lax.optimization_barrier(jnp.sum(selected, axis=1, keepdims=True))
    sent = low_back(jnp.broadcast_to(ffn_normed[:, None, :], (token_length, TOP, MODEL_DIMENSION)))
    routed = experts(sent, route, expert_in, expert_out)
    mixture = lax.optimization_barrier(jnp.sum(gates[:, :, None] * routed, axis=1))
    return middle + mixture

def reference(hidden_in, out_grad, doc_lengths, routes, attention_input_weight, attn_out_weight, norm_gains, head_gains, router_weight, expert_in, expert_out):
    params = tuple((p.astype(jnp.float32) for p in (attention_input_weight, attn_out_weight, norm_gains, head_gains, router_weight, expert_in, expert_out)))
    zero_grads = jax.tree.map(jnp.zeros_like, params)

    def per_sequence(totals, scan_item):
        hidden, upstream, lengths, route = scan_item

        def forward(hidden_f, *weights):
            return layer(hidden_f, *weights, lengths, route)
        result, pullback = jax.vjp(forward, hidden.astype(jnp.float32), *params)
        grads = pullback(upstream.astype(jnp.float32))
        totals = jax.tree.map(lambda a, b: a + b, totals, tuple(grads[1:]))
        return (totals, (result.astype(jnp.bfloat16), grads[0].astype(jnp.bfloat16)))
    totals, (outputs, input_grads) = lax.scan(per_sequence, zero_grads, (hidden_in, out_grad, doc_lengths, routes))
    return (outputs, input_grads, totals[0], totals[1], totals[2], totals[3], totals[4], totals[5], totals[6])
```

```python
import functools

import jax
import jax.numpy as jnp
from jax import lax
from jax.experimental import pallas as pl
from jax.experimental.pallas import tpu as pltpu
from jax.sharding import PartitionSpec as P

epsilon = 1e-06
rotary_base = 1000000.0
key_span = 512


def doc_tables(lengths, positions):
    doc_ends = jnp.cumsum(lengths)
    passed = positions[:, None] >= doc_ends[None, :]
    doc_index = jnp.sum(passed.astype(jnp.int32), axis=1)
    first_pos = jnp.sum(jnp.where(passed, lengths[None, :], 0), axis=1)
    return (doc_index, positions - first_pos)


def rotate(values, relative, sign):
    half_dim = values.shape[-1] // 2
    freqs = rotary_base ** (-2.0 * jnp.arange(half_dim, dtype=jnp.float32) / values.shape[-1])
    angles = relative.astype(jnp.float32)[:, None] * freqs[None, :]
    cosine = jnp.cos(angles)[:, None, :]
    sine = sign * jnp.sin(angles)[:, None, :]
    first = values[..., :half_dim]
    second = values[..., half_dim:]
    return jnp.concatenate(
        [first * cosine - second * sine, second * cosine + first * sine], axis=-1
    )


def norm_forward(values, gain_vec):
    scale_vec = lax.rsqrt(jnp.mean(values * values, axis=-1, keepdims=True) + epsilon)
    unit_vec = values * scale_vec
    return (unit_vec * gain_vec, unit_vec, scale_vec)


def norm_backward(upstream, unit_vec, scale_vec, gain_vec):
    along = upstream * gain_vec
    return scale_vec * (along - unit_vec * jnp.mean(along * unit_vec, axis=-1, keepdims=True))


def per_device_general(
    hidden_in,
    out_grad,
    doc_lengths,
    routes,
    attention_input_weight,
    attn_out_weight,
    norm_gains,
    head_gains,
    router_weight,
    expert_in,
    expert_out,
):
    hidden = hidden_in[0].astype(jnp.float32)
    tokens_here, model_width = hidden.shape
    head_dim = head_gains.shape[0]
    expert_count = router_weight.shape[1]
    local_experts = expert_in.shape[1]
    route_picks = routes.shape[2]
    cycle_size = lax.axis_size("ctx")
    cycle_place = lax.axis_index("ctx")
    seq_length = tokens_here * cycle_size
    lengths = doc_lengths[0]
    query_pos = cycle_place * tokens_here + jnp.arange(tokens_here, dtype=jnp.int32)
    query_doc, query_rel = doc_tables(lengths, query_pos)
    gain_attn = norm_gains[:, 0].astype(jnp.float32)
    gain_ffn = norm_gains[:, 1].astype(jnp.float32)
    gain_query = head_gains[:, 0].astype(jnp.float32)
    gain_key = head_gains[:, 1].astype(jnp.float32)
    normed, hidden_unit, hidden_scale = norm_forward(hidden, gain_attn)
    normed_low = normed.astype(jnp.bfloat16)
    weight_in, weight_out = (
        lax.all_gather(attention_input_weight, ("ctx", "exp"), axis=0, tiled=True),
        lax.all_gather(attn_out_weight, ("ctx", "exp"), axis=0, tiled=True),
    )
    joined_projection = jnp.dot(normed_low, weight_in, preferred_element_type=jnp.float32)
    joined_width = weight_in.shape[1]
    query_width = weight_out.shape[1]
    head_count = query_width // head_dim
    kv_width = (joined_width - query_width) // 2
    kv_heads = kv_width // head_dim
    query_group_size = head_count // kv_heads
    query_raw = joined_projection[:, :query_width].reshape(tokens_here, head_count, head_dim)
    key_raw = joined_projection[:, query_width : query_width + kv_width].reshape(
        tokens_here, kv_heads, head_dim
    )
    value_low = joined_projection[:, query_width + kv_width :].astype(jnp.bfloat16)
    query_normed, query_unit, query_scale = norm_forward(query_raw, gain_query)
    key_normed, key_unit, key_scale = norm_forward(key_raw, gain_key)
    query_low = rotate(query_normed, query_rel, 1.0).astype(jnp.bfloat16)
    key_low = rotate(key_normed, query_rel, 1.0).astype(jnp.bfloat16)
    keys_local = jnp.stack([key_low.reshape(tokens_here, kv_width), value_low], axis=1)
    keys_all, in_all, out_all = (
        lax.all_gather(keys_local, "ctx", axis=0, tiled=True),
        lax.all_gather(expert_in, "ctx", axis=0, tiled=True),
        lax.all_gather(expert_out, "ctx", axis=0, tiled=True),
    )
    span = min(key_span, seq_length)
    block_count = seq_length // span
    key_blocks = keys_all.reshape(block_count, span, 2, kv_heads, head_dim)
    block_ids = jnp.arange(block_count, dtype=jnp.int32)
    query_rows = (
        query_low.reshape(tokens_here, kv_heads, query_group_size, head_dim)
        .transpose(1, 2, 0, 3)
        .reshape(kv_heads, query_group_size * tokens_here, head_dim)
    )
    score_scale = head_dim ** (-0.5)

    def block_scores(block_id, key_block):
        raw_scores = (
            jnp.einsum(
                "hrd,khd->hrk", query_rows, key_block[:, 0], preferred_element_type=jnp.float32
            )
            * score_scale
        )
        key_pos = block_id * span + jnp.arange(span, dtype=jnp.int32)
        key_doc = doc_tables(lengths, key_pos)[0]
        allowed = (key_pos[None, :] <= query_pos[:, None]) & (
            key_doc[None, :] == query_doc[:, None]
        )
        allowed = jnp.tile(allowed, (query_group_size, 1))[None]
        return (jnp.where(allowed, raw_scores, -1e30), allowed)

    def stats_step(running, scan_item):
        best_score, mass_sum = running
        block_id, key_block = scan_item
        masked, allowed = block_scores(block_id, key_block)
        new_best = jnp.maximum(best_score, jnp.max(masked, axis=-1))
        fresh = jnp.sum(jnp.where(allowed, jnp.exp(masked - new_best[..., None]), 0.0), axis=-1)
        return ((new_best, mass_sum * jnp.exp(best_score - new_best) + fresh), None)

    start_best = jnp.full((kv_heads, query_group_size * tokens_here), -1e30, jnp.float32)
    (best_score, mass_sum), unused = lax.scan(
        stats_step, (start_best, jnp.zeros_like(start_best)), (block_ids, key_blocks)
    )
    log_total = best_score + jnp.log(mass_sum)

    def value_step(summed, scan_item):
        block_id, key_block = scan_item
        masked, allowed = block_scores(block_id, key_block)
        weights = jnp.where(allowed, jnp.exp(masked - log_total[..., None]), 0.0).astype(
            jnp.bfloat16
        )
        return (
            summed
            + jnp.einsum(
                "hrk,khd->hrd", weights, key_block[:, 1], preferred_element_type=jnp.float32
            ),
            None,
        )

    start_rows = jnp.zeros((kv_heads, query_group_size * tokens_here, head_dim), jnp.float32)
    attended, unused = lax.scan(value_step, start_rows, (block_ids, key_blocks))
    attended_low = (
        attended.reshape(kv_heads, query_group_size, tokens_here, head_dim)
        .transpose(2, 0, 1, 3)
        .reshape(tokens_here, query_width)
        .astype(jnp.bfloat16)
    )
    branch = jnp.einsum("rc,dc->rd", attended_low, weight_out, preferred_element_type=jnp.float32)
    middle = hidden + branch
    ffn_normed, middle_unit, middle_scale = norm_forward(middle, gain_ffn)
    ffn_low = ffn_normed.astype(jnp.bfloat16)
    logits = jnp.dot(ffn_low, router_weight, preferred_element_type=jnp.float32)
    probs = jax.nn.softmax(logits, axis=-1)
    route_here = routes[0]
    route_hits = (
        route_here[:, :, None] == jnp.arange(expert_count, dtype=jnp.int32)[None, None, :]
    ).astype(jnp.float32)
    selected = jnp.sum(route_hits * probs[:, None, :], axis=-1)
    sel_total = jnp.sum(selected, axis=1, keepdims=True)
    gates = selected / sel_total
    capacity = 5 * tokens_here * route_picks // (4 * expert_count)
    flat_route = route_here.reshape(-1)
    slot_hits = (flat_route[:, None] == jnp.arange(expert_count, dtype=jnp.int32)[None, :]).astype(
        jnp.int32
    )
    slot_index = jnp.sum((jnp.cumsum(slot_hits, axis=0) - slot_hits) * slot_hits, axis=1)
    target = flat_route * capacity + slot_index
    exp_size = lax.axis_size("exp")
    buffer_shape = (exp_size, local_experts * capacity, model_width)
    arrive_shape = (exp_size, local_experts, capacity, model_width)
    empty_buffer = jnp.zeros((expert_count * capacity, model_width), jnp.bfloat16)
    outgoing = empty_buffer.at[target].set(jnp.repeat(ffn_low, route_picks, axis=0))
    arrived = lax.all_to_all(
        outgoing.reshape(buffer_shape), "exp", split_axis=0, concat_axis=0, tiled=True
    ).reshape(arrive_shape)
    gate_up = jnp.einsum("secd,dekf->seckf", arrived, in_all, preferred_element_type=jnp.float32)
    gate_part = gate_up[:, :, :, 0]
    up_part = gate_up[:, :, :, 1]
    sigmoid_part = jax.nn.sigmoid(gate_part)
    silu_part = jax.nn.silu(gate_part)
    act_low = (silu_part * up_part).astype(jnp.bfloat16)
    made = jnp.einsum(
        "secf,def->secd", act_low, out_all, preferred_element_type=jnp.float32
    ).astype(jnp.bfloat16)
    returned = lax.all_to_all(
        made.reshape(buffer_shape), "exp", split_axis=0, concat_axis=0, tiled=True
    ).reshape(expert_count * capacity, model_width)
    route_out = returned[target].astype(jnp.float32).reshape(tokens_here, route_picks, model_width)
    mixture = jnp.sum(gates[:, :, None] * route_out, axis=1)
    output = (middle + mixture).astype(jnp.bfloat16)[None]
    upstream = out_grad[0].astype(jnp.float32)
    gate_grads = jnp.sum(upstream[:, None, :] * route_out, axis=-1)
    route_grads = (
        (gates[:, :, None] * upstream[:, None, :])
        .astype(jnp.bfloat16)
        .reshape(tokens_here * route_picks, model_width)
    )
    outgoing_grads = empty_buffer.at[target].set(route_grads)
    grads_arrived = lax.all_to_all(
        outgoing_grads.reshape(buffer_shape), "exp", split_axis=0, concat_axis=0, tiled=True
    ).reshape(arrive_shape)
    act_grads = jnp.einsum(
        "secd,def->secf", grads_arrived, out_all, preferred_element_type=jnp.float32
    )
    gate_grad_part = act_grads * up_part * sigmoid_part * (1.0 + gate_part * (1.0 - sigmoid_part))
    gate_up_grads = jnp.stack([gate_grad_part, act_grads * silu_part], axis=3).astype(jnp.bfloat16)
    input_rows = jnp.einsum(
        "seckf,dekf->secd", gate_up_grads, in_all, preferred_element_type=jnp.float32
    ).astype(jnp.bfloat16)
    came_back = lax.all_to_all(
        input_rows.reshape(buffer_shape), "exp", split_axis=0, concat_axis=0, tiled=True
    ).reshape(expert_count * capacity, model_width)
    sent_grads = jnp.sum(
        came_back[target].astype(jnp.float32).reshape(tokens_here, route_picks, model_width), axis=1
    )
    term_in = jnp.einsum(
        "secd,seckf->dekf", arrived, gate_up_grads, preferred_element_type=jnp.float32
    )
    term_out = jnp.einsum(
        "secd,secf->def", grads_arrived, act_low, preferred_element_type=jnp.float32
    )
    expert_local = lax.psum_scatter(
        jnp.concatenate([term_in, term_out[:, :, None, :]], axis=2).astype(jnp.bfloat16),
        "ctx",
        scatter_dimension=0,
        tiled=True,
    )
    weighted = jnp.sum(gate_grads * gates, axis=1, keepdims=True)
    sel_grads = (gate_grads - weighted) / sel_total
    prob_grads = jnp.sum(sel_grads[:, :, None] * route_hits, axis=1)
    logit_grads = probs * (prob_grads - jnp.sum(probs * prob_grads, axis=1, keepdims=True))
    router_float = router_weight.astype(jnp.float32)
    ffn_grads = sent_grads + jnp.dot(logit_grads, router_float.T, precision=lax.Precision.HIGHEST)
    router_grads = jnp.dot(
        ffn_low.astype(jnp.float32).T, logit_grads, precision=lax.Precision.HIGHEST
    )
    middle_grad = upstream + norm_backward(ffn_grads, middle_unit, middle_scale, gain_ffn)
    attn_grad_low = middle_grad.astype(jnp.bfloat16)
    heads_grad_low = jnp.dot(attn_grad_low, weight_out, preferred_element_type=jnp.float32).astype(
        jnp.bfloat16
    )
    grad_rows = (
        heads_grad_low.reshape(tokens_here, kv_heads, query_group_size, head_dim)
        .transpose(1, 2, 0, 3)
        .reshape(kv_heads, query_group_size * tokens_here, head_dim)
    )

    def delta_step(summed, scan_item):
        block_id, key_block = scan_item
        masked, allowed = block_scores(block_id, key_block)
        weights = jnp.where(allowed, jnp.exp(masked - log_total[..., None]), 0.0)
        weight_grads = jnp.einsum(
            "hrd,khd->hrk", grad_rows, key_block[:, 1], preferred_element_type=jnp.float32
        )
        return (summed + jnp.sum(weights * weight_grads, axis=-1), None)

    delta_sum, unused = lax.scan(delta_step, jnp.zeros_like(log_total), (block_ids, key_blocks))

    def grad_step(query_grads, scan_item):
        block_id, key_block = scan_item
        masked, allowed = block_scores(block_id, key_block)
        weights = jnp.where(allowed, jnp.exp(masked - log_total[..., None]), 0.0)
        weight_grads = jnp.einsum(
            "hrd,khd->hrk", grad_rows, key_block[:, 1], preferred_element_type=jnp.float32
        )
        score_grads = (weights * (weight_grads - delta_sum[..., None])).astype(jnp.bfloat16)
        query_grads = (
            query_grads
            + jnp.einsum(
                "hrk,khd->hrd", score_grads, key_block[:, 0], preferred_element_type=jnp.float32
            )
            * score_scale
        )
        key_grads = (
            jnp.einsum("hrk,hrd->khd", score_grads, query_rows, preferred_element_type=jnp.float32)
            * score_scale
        )
        value_grads = jnp.einsum(
            "hrk,hrd->khd",
            weights.astype(jnp.bfloat16),
            grad_rows,
            preferred_element_type=jnp.float32,
        )
        return (query_grads, jnp.stack([key_grads, value_grads], axis=1))

    query_grads, block_grads = lax.scan(grad_step, start_rows, (block_ids, key_blocks))
    key_value_grads = lax.psum_scatter(
        block_grads.reshape(seq_length, 2, kv_width).astype(jnp.bfloat16),
        "ctx",
        scatter_dimension=0,
        tiled=True,
    ).astype(jnp.float32)
    query_grads = (
        query_grads.reshape(kv_heads, query_group_size, tokens_here, head_dim)
        .transpose(2, 0, 1, 3)
        .reshape(tokens_here, head_count, head_dim)
    )
    query_turned = rotate(query_grads, query_rel, -1.0)
    query_proj = norm_backward(query_turned, query_unit, query_scale, gain_query)
    key_turned = rotate(
        key_value_grads[:, 0].reshape(tokens_here, kv_heads, head_dim), query_rel, -1.0
    )
    key_proj = norm_backward(key_turned, key_unit, key_scale, gain_key)
    head_gain_grads = jnp.stack(
        [
            jnp.sum(query_turned * query_unit, axis=(0, 1)),
            jnp.sum(key_turned * key_unit, axis=(0, 1)),
        ],
        axis=1,
    )
    joined_grads = jnp.concatenate(
        [
            query_proj.reshape(tokens_here, query_width),
            key_proj.reshape(tokens_here, kv_width),
            key_value_grads[:, 1],
        ],
        axis=1,
    ).astype(jnp.bfloat16)
    normed_grads = jnp.einsum(
        "rc,dc->rd", joined_grads, weight_in, preferred_element_type=jnp.float32
    )
    input_part = norm_backward(normed_grads, hidden_unit, hidden_scale, gain_attn)
    input_grad = (middle_grad + input_part).astype(jnp.bfloat16)[None]
    norm_gain_grads = jnp.stack(
        [jnp.sum(normed_grads * hidden_unit, axis=0), jnp.sum(ffn_grads * middle_unit, axis=0)],
        axis=1,
    )
    norm_total, head_total, router_total = lax.psum(
        (norm_gain_grads, head_gain_grads, router_grads), ("grp", "ctx", "exp")
    )
    part_in = jnp.einsum("rc,rq->cq", normed_low, joined_grads, preferred_element_type=jnp.float32)
    part_out = jnp.einsum(
        "rc,rq->cq", attn_grad_low, attended_low, preferred_element_type=jnp.float32
    )
    dense_local = lax.psum_scatter(
        jnp.concatenate([part_in, part_out], axis=1),
        ("ctx", "exp"),
        scatter_dimension=0,
        tiled=True,
    )
    dense_total, expert_total = (
        lax.psum(dense_local.astype(jnp.bfloat16), "grp").astype(jnp.float32),
        lax.psum(expert_local, "grp").astype(jnp.float32),
    )
    return (
        output,
        input_grad,
        dense_total[:, :joined_width],
        dense_total[:, joined_width:],
        norm_total,
        head_total,
        router_total,
        expert_total[:, :, :2],
        expert_total[:, :, 2],
    )


NT = (((1,), (1,)), ((), ()))

def head_norm(raw):
    scale = lax.rsqrt(jnp.mean(raw * raw, axis=-1, keepdims=True) + epsilon)
    return raw * scale, scale

def turn(values, cosine, sine):
    return values * cosine + pltpu.roll(values, values.shape[-1] // 2, 1) * sine

def dots(a, b):
    return jnp.dot(a, b, preferred_element_type=jnp.float32)

def dots_nt(a, b):
    return lax.dot_general(a, b, NT, preferred_element_type=jnp.float32)

def allowed_chunk(start, i, j, tile):
    key_pos = j * tile + lax.broadcasted_iota(jnp.int32, (tile, tile), 0)
    ok = key_pos >= start
    if i == j:
        query_pos = i * tile + lax.broadcasted_iota(jnp.int32, (tile, tile), 1)
        ok = ok & (key_pos <= query_pos)
    return ok

def attend_kernel(tile, q_ref, k_ref, v_ref, cos_ref, sin_ref, start_ref, gain_ref,
                  o_ref, lse_ref, key_s, value_t):
    length, head_dim = q_ref.shape
    c = head_dim ** -0.5 * 1.4426950408889634
    @pl.when(pl.program_id(0) == 0)
    def _():
        unit, _ = head_norm(k_ref[...])
        key_s[...] = turn(unit * gain_ref[1:2], cos_ref[...], sin_ref[...]).astype(jnp.bfloat16)
        value_t[...] = v_ref[...].T.astype(jnp.bfloat16)
    unit, _ = head_norm(q_ref[...])
    query = turn(unit * gain_ref[0:1], cos_ref[...], sin_ref[...]).astype(jnp.bfloat16)
    for i in range(length // tile):
        rows = slice(i * tile, (i + 1) * tile)
        start = start_ref[:, rows]
        mass = jnp.zeros((1, tile), jnp.float32)
        total = jnp.zeros((head_dim, tile), jnp.float32)
        for j in range(i + 1):
            cols = slice(j * tile, (j + 1) * tile)
            s = dots_nt(key_s[cols, :], query[rows])
            p = jnp.where(allowed_chunk(start, i, j, tile), jnp.exp2(s * c), 0.0)
            mass = mass + jnp.sum(p, axis=0, keepdims=True)
            total = total + dots(value_t[:, cols], p.astype(jnp.bfloat16))
        o_ref[rows, :] = (total / mass).T.astype(jnp.bfloat16)
        lse_ref[0, :, rows] = jnp.log2(mass)

def attend(qkv, cosine, sine, start, gains, heads):
    length, head_dim = cosine.shape
    full = lambda shape: pl.BlockSpec(shape, lambda h: (0, 0))
    col = lambda at: pl.BlockSpec((length, head_dim), lambda h: (0, at))
    return pl.pallas_call(
        functools.partial(attend_kernel, min(256, length)),
        grid=(heads,),
        in_specs=[
            pl.BlockSpec((length, head_dim), lambda h: (0, h)), col(heads), col(heads + 1),
            full((length, head_dim)), full((length, head_dim)), full((1, length)), full(gains.shape),
        ],
        out_specs=[
            pl.BlockSpec((length, head_dim), lambda h: (0, h)),
            pl.BlockSpec((1, 1, length), lambda h: (h, 0, 0)),
        ],
        out_shape=[
            jax.ShapeDtypeStruct((length, heads * head_dim), jnp.bfloat16),
            jax.ShapeDtypeStruct((heads, 1, length), jnp.float32),
        ],
        scratch_shapes=[
            pltpu.VMEM((length, head_dim), jnp.bfloat16),
            pltpu.VMEM((head_dim, length), jnp.bfloat16),
        ],
        compiler_params=pltpu.CompilerParams(vmem_limit_bytes=48 * 2**20),
    )(qkv, qkv, qkv, cosine, sine, start, gains)

def attend_back_kernel(tile, heads, q_ref, k_ref, v_ref, cos_ref, sin_ref, start_ref, gain_ref,
                       o_ref, go_ref, lse_ref, grad_ref, gain_grad_ref,
                       key_s, key_t, value_s, key_grad, value_grad, query_grad):
    length, head_dim = q_ref.shape
    scale = head_dim ** -0.5
    c = scale * 1.4426950408889634
    step = pl.program_id(0)

    def norm_back(turned_grad, raw, row):
        back = turn(turned_grad, cos_ref[...], -sin_ref[...])
        unit, unit_scale = head_norm(raw)
        gain_grad_ref[row:row + 1] += jnp.sum(back * unit, axis=0, keepdims=True)
        along = back * gain_ref[row:row + 1]
        return unit_scale * (along - unit * jnp.mean(along * unit, axis=-1, keepdims=True))

    @pl.when(step == 0)
    def _():
        unit, _ = head_norm(k_ref[...])
        key = turn(unit * gain_ref[1:2], cos_ref[...], sin_ref[...])
        key_s[...] = key.astype(jnp.bfloat16)
        key_t[...] = key.T.astype(jnp.bfloat16)
        value_s[...] = v_ref[...].astype(jnp.bfloat16)
        key_grad[...] = jnp.zeros_like(key_grad)
        value_grad[...] = jnp.zeros_like(value_grad)
        gain_grad_ref[...] = jnp.zeros_like(gain_grad_ref)

    @pl.when(step < heads)
    def _():
        unit, _ = head_norm(q_ref[...])
        query = turn(unit * gain_ref[0:1], cos_ref[...], sin_ref[...]).astype(jnp.bfloat16)
        for i in range(length // tile):
            rows = slice(i * tile, (i + 1) * tile)
            start = start_ref[:, rows]
            lse = lse_ref[0, :, rows]
            up = go_ref[rows, :]
            delta = jnp.sum((up.astype(jnp.float32) * o_ref[rows, :].astype(jnp.float32)).T, axis=0, keepdims=True)
            q_i = query[rows]
            total = jnp.zeros((head_dim, tile), jnp.float32)
            for j in range(i + 1):
                cols = slice(j * tile, (j + 1) * tile)
                s = dots_nt(key_s[cols, :], q_i)
                p = jnp.where(allowed_chunk(start, i, j, tile), jnp.exp2(s * c - lse), 0.0)
                dp = dots_nt(value_s[cols, :], up)
                ds = (p * (dp - delta)).astype(jnp.bfloat16)
                value_grad[cols, :] += dots(p.astype(jnp.bfloat16), up)
                key_grad[cols, :] += dots(ds, q_i)
                total = total + dots(key_t[:, cols], ds)
            query_grad[rows, :] = (total * scale).T
        grad_ref[...] = norm_back(query_grad[...], q_ref[...], 0).astype(jnp.bfloat16)

    @pl.when(step == heads)
    def _():
        grad_ref[...] = norm_back(key_grad[...] * scale, k_ref[...], 1).astype(jnp.bfloat16)

    @pl.when(step == heads + 1)
    def _():
        grad_ref[...] = value_grad[...].astype(jnp.bfloat16)

def attend_back(qkv, cosine, sine, start, gains, attended, upstream, lse, heads):
    length, head_dim = cosine.shape
    full = lambda shape: pl.BlockSpec(shape, lambda h: (0, 0))
    col = lambda at: pl.BlockSpec((length, head_dim), lambda h: (0, at))
    per_head = pl.BlockSpec((length, head_dim), lambda h: (0, jnp.minimum(h, heads - 1)))
    return pl.pallas_call(
        functools.partial(attend_back_kernel, min(256, length), heads),
        grid=(heads + 2,),
        in_specs=[
            per_head, col(heads), col(heads + 1),
            full((length, head_dim)), full((length, head_dim)), full((1, length)), full(gains.shape),
            per_head, per_head,
            pl.BlockSpec((1, 1, length), lambda h: (jnp.minimum(h, heads - 1), 0, 0)),
        ],
        out_specs=[
            pl.BlockSpec((length, head_dim), lambda h: (0, h)),
            full((8, head_dim)),
        ],
        out_shape=[
            jax.ShapeDtypeStruct((length, (heads + 2) * head_dim), jnp.bfloat16),
            jax.ShapeDtypeStruct((8, head_dim), jnp.float32),
        ],
        scratch_shapes=[
            pltpu.VMEM((length, head_dim), jnp.bfloat16),
            pltpu.VMEM((head_dim, length), jnp.bfloat16),
            pltpu.VMEM((length, head_dim), jnp.bfloat16),
            pltpu.VMEM((length, head_dim), jnp.float32),
            pltpu.VMEM((length, head_dim), jnp.float32),
            pltpu.VMEM((length, head_dim), jnp.float32),
        ],
        compiler_params=pltpu.CompilerParams(vmem_limit_bytes=48 * 2**20),
    )(qkv, qkv, qkv, cosine, sine, start, gains, attended, upstream, lse)


low = jnp.bfloat16


def swap_on(value, axis, mask):
    count = lax.axis_size(axis)
    return lax.ppermute(value, axis, [(i, i ^ mask) for i in range(count)])


def line_gather(block, axis):
    n = lax.axis_size(axis)
    rights, lefts = [block], [block]
    for s in range(1, n):
        rights.append(lax.ppermute(rights[-1], axis, [(i, i + 1) for i in range(s - 1, n - 1)]))
        lefts.append(lax.ppermute(lefts[-1], axis, [(i, i - 1) for i in range(1, n - s + 1)]))
    return [block] + [rights[s] + lefts[n - s] for s in range(1, n)]


def line_scatter(parts, axis):
    n = lax.axis_size(axis)
    right = left = None
    for s in range(1, n):
        to_right = parts[n - s] if right is None else add_low(parts[n - s], right)
        to_left = parts[s] if left is None else add_low(parts[s], left)
        right = lax.ppermute(to_right, axis, [(i, i + 1) for i in range(s)])
        left = lax.ppermute(to_left, axis, [(i, i - 1) for i in range(n - s, n)])
    return parts[0].astype(jnp.float32) + right.astype(jnp.float32) + left.astype(jnp.float32)


def add_low(a, b):
    return (a.astype(jnp.float32) + b.astype(jnp.float32)).astype(low)


def pick(array, index):
    return lax.dynamic_index_in_dim(array, index, 0, keepdims=False)


def per_device(
    hidden_in,
    out_grad,
    doc_lengths,
    routes,
    attention_input_weight,
    attn_out_weight,
    norm_gains,
    head_gains,
    router_weight,
    expert_in,
    expert_out,
):
    hidden = hidden_in[0].astype(jnp.float32)
    rows, width = hidden.shape
    head_dim = head_gains.shape[0]
    expert_count = router_weight.shape[1]
    top = routes.shape[2]
    n_ctx, n_exp = lax.axis_size("ctx"), lax.axis_size("exp")
    grp, ctx, exp = lax.axis_index("grp"), lax.axis_index("ctx"), lax.axis_index("exp")
    half, core = ctx // 2, ctx % 2
    length = rows * n_ctx
    query_width = attn_out_weight.shape[1]
    kv_width = (attention_input_weight.shape[1] - query_width) // 2
    heads = query_width // head_dim // n_ctx
    shard = attention_input_weight.shape[0]
    f32 = jnp.float32

    def dot(a, b):
        return jnp.dot(a, b, preferred_element_type=f32)

    def dot_nt(a, b):
        return lax.dot_general(a, b, (((1,), (1,)), ((), ())), preferred_element_type=f32)

    def dot_tn(a, b):
        return lax.dot_general(a, b, (((0,), (0,)), ((), ())), preferred_element_type=f32)

    def by_exp(a):
        return a.reshape(a.shape[0], n_ctx, n_exp, shard).transpose(0, 2, 1, 3).reshape(a.shape)

    def by_ctx(a):
        return a.reshape(a.shape[0], n_exp, n_ctx, shard).transpose(0, 2, 1, 3).reshape(a.shape)

    def own_half_first(a):
        return jnp.where(half == 0, a, jnp.concatenate([a[:, width // 2 :], a[:, : width // 2]], 1))

    def gather_ctx(block):
        over = swap_on(block, "ctx", 2)
        blocks = [block, swap_on(block, "ctx", 1), over, swap_on(over, "ctx", 1)]
        return place_ctx(blocks)

    def place_ctx(blocks):
        out = jnp.zeros((n_ctx,) + blocks[0].shape, blocks[0].dtype)
        for m in range(n_ctx):
            out = lax.dynamic_update_index_in_dim(out, blocks[m], ctx ^ m, 0)
        return out

    def scatter_ctx(parts):
        got = swap_on(jnp.stack([pick(parts, ctx ^ 1), pick(parts, ctx ^ 3)]), "ctx", 1)
        mine = pick(parts, ctx).astype(f32) + got[0].astype(f32)
        other = add_low(pick(parts, ctx ^ 2), got[1])
        return mine + swap_on(other, "ctx", 2).astype(f32)

    positions = jnp.arange(length, dtype=jnp.int32)
    relative = doc_tables(doc_lengths[0], positions)[1]
    doc_start = (positions - relative)[None, :]
    freqs = rotary_base ** (-2.0 * jnp.arange(head_dim // 2, dtype=f32) / head_dim)
    angles = relative.astype(f32)[:, None] * freqs[None, :]
    cosine = jnp.concatenate([jnp.cos(angles)] * 2, 1)
    sine = jnp.concatenate([-jnp.sin(angles), jnp.sin(angles)], 1)
    gains = jnp.pad(head_gains.astype(f32).T, ((0, 6), (0, 0)))
    gain_attn = norm_gains[:, 0].astype(f32)
    gain_ffn = norm_gains[:, 1].astype(f32)

    def weight_in_of(at):
        return jnp.concatenate(
            [
                lax.dynamic_slice_in_dim(attention_input_weight, at * heads * head_dim, heads * head_dim, 1),
                lax.dynamic_slice_in_dim(attention_input_weight, query_width + at * head_dim, head_dim, 1),
                lax.dynamic_slice_in_dim(
                    attention_input_weight, query_width + kv_width + at * head_dim, head_dim, 1
                ),
            ],
            1,
        )

    def weight_out_of(at):
        return lax.dynamic_slice_in_dim(attn_out_weight, at * heads * head_dim, heads * head_dim, 1)

    def all_rows(piece_of):
        blocks = [piece_of(ctx)] + [swap_on(piece_of(ctx ^ m), "ctx", m) for m in range(1, n_ctx)]
        block = place_ctx(blocks)
        blocks = line_gather(block, "exp")
        out = jnp.zeros((n_exp,) + block.shape, block.dtype)
        for s in range(n_exp):
            out = lax.dynamic_update_index_in_dim(out, blocks[s], (exp - s) % n_exp, 0)
        return out.reshape(width, block.shape[-1])

    normed, hidden_unit, hidden_scale = norm_forward(hidden, gain_attn)
    normed_seq = gather_ctx(by_exp(normed.astype(low))).reshape(length, width)
    weight_in = all_rows(weight_in_of)
    weight_out = all_rows(weight_out_of)

    capacity = 5 * rows * top // (4 * expert_count)
    hits = jnp.any(routes[0][:, :, None] == jnp.arange(expert_count, dtype=jnp.int32), axis=1)
    before = jnp.tril(jnp.ones((rows, rows), low), -1)
    slots = jnp.where(hits, dot(before, hits.astype(low)), -1.0).T
    slots_all = lax.all_gather(slots, ("ctx", "exp"), axis=0).reshape(n_ctx, n_exp, expert_count, rows)
    order = [(s, j) for s in range(n_exp) for j in range(2)]
    slots_of = jnp.stack([pick(pick(slots_all, ctx ^ j), (exp - s) % n_exp) for s, j in order])

    local_experts = expert_in.shape[1]
    hidden_units = expert_out.shape[2]
    quarter = expert_in.shape[0]

    def expert_rows(at):
        return jnp.concatenate(
            [
                lax.dynamic_index_in_dim(expert_in, at, 1, keepdims=False).reshape(quarter, -1),
                lax.dynamic_index_in_dim(expert_out, at, 1, keepdims=False),
            ],
            1,
        )

    here = [2 * core + (1 - grp), 2 * core + grp]
    there = [2 * (1 - core) + (1 - grp), 2 * (1 - core) + grp]
    over_same = swap_on(expert_rows(here[0]), "ctx", 2)
    over_other = swap_on(expert_rows(there[0]), "ctx", 3)
    expert_weights = []
    for j in range(2):
        same, other = expert_rows(here[j]), swap_on(expert_rows(there[j]), "ctx", 1)
        if j == 1:
            over_same, over_other = swap_on(over_same, "grp", 1), swap_on(over_other, "grp", 1)
        expert_weights.append(
            jnp.concatenate(
                [
                    jnp.where(core == 0, same, other),
                    jnp.where(core == 0, other, same),
                    jnp.where(core == 0, over_same, over_other),
                    jnp.where(core == 0, over_other, over_same),
                ]
            )
        )

    def gather_tokens(block):
        blocks = line_gather(block, "exp")
        return jnp.stack([b for own in blocks for b in (own, swap_on(own, "ctx", 1))])

    qkv = dot(normed_seq, weight_in)
    attended, log_mass = attend(qkv, cosine, sine, doc_start, gains, heads)
    branch = dot_nt(attended, weight_out).astype(low).reshape(n_ctx, rows, width)
    middle = hidden + by_ctx(scatter_ctx(branch))
    ffn_normed, middle_unit, middle_scale = norm_forward(middle, gain_ffn)
    ffn_low = ffn_normed.astype(low)

    tokens = gather_tokens(own_half_first(ffn_low))
    upstreams = gather_tokens(own_half_first(out_grad[0]))
    router_here = jnp.where(
        half == 0, router_weight, jnp.concatenate([router_weight[width // 2 :], router_weight[: width // 2]])
    )
    logits = dot(tokens.reshape(-1, width), router_here)
    probs_all = jax.nn.softmax(logits, axis=-1).reshape(len(order), rows, expert_count)
    selected = jnp.where(slots_of.transpose(0, 2, 1) >= 0, probs_all, 0.0)
    sel_sums = jnp.sum(selected, axis=-1, keepdims=True)
    gates_all = selected / sel_sums
    probs, sel_total = probs_all[0], sel_sums[0]
    gates = gates_all[0]

    mixed, sent, tables, gate_grad_parts, grad_halves = [], [], [], [], []
    for j in range(2):
        expert = exp * local_experts + here[j]
        slot = lax.dynamic_index_in_dim(slots_of, expert, 1, keepdims=False)
        table = slot[:, None, :] == jnp.arange(capacity, dtype=f32)[None, :, None]
        gate_rows = lax.dynamic_index_in_dim(gates_all, expert, 2, keepdims=False)
        gate_slots = jnp.sum(jnp.where(table, gate_rows[:, None, :], 0.0), axis=-1)
        table_low = table.astype(low)
        gather = lambda a: jnp.einsum(
            "bct,btd->bcd", table_low, a, preferred_element_type=f32
        ).reshape(-1, width)
        inputs = gather(tokens).astype(low)
        ups = gather(upstreams)
        grads = (ups * gate_slots.reshape(-1, 1)).astype(low)
        weight = expert_weights[j]
        into, outof = weight[:, : 2 * hidden_units], weight[:, 2 * hidden_units :]
        gate_up = dot(inputs, into)
        gate_part, up_part = gate_up[:, :hidden_units], gate_up[:, hidden_units:]
        sigmoid_part = jax.nn.sigmoid(gate_part)
        silu_part = gate_part * sigmoid_part
        act = (silu_part * up_part).astype(low)
        made = dot_nt(act, outof).astype(low)
        act_grad = dot(grads, outof)
        gate_grad = act_grad * up_part * sigmoid_part * (1.0 + gate_part * (1.0 - sigmoid_part))
        gate_up_grad = jnp.concatenate([gate_grad, act_grad * silu_part], 1).astype(low)
        sent.append(dot_nt(gate_up_grad, into).astype(low).reshape(len(order), capacity, width))
        gate_grad_slots = jnp.sum(ups * made.astype(f32), axis=-1).reshape(len(order), capacity)
        gate_grad_parts.append(jnp.sum(jnp.where(table, gate_grad_slots[:, :, None], 0.0), axis=1))
        mixed.append(
            (made.astype(f32) * gate_slots.reshape(-1, 1)).astype(low).reshape(len(order), capacity, width)
        )
        tables.append(table_low)
        grad = jnp.concatenate([dot_tn(inputs, gate_up_grad), dot_tn(grads, act)], 1).astype(low)
        grad_halves.append(
            grad[: width // 2].astype(f32) + swap_on(grad[width // 2 :], "ctx", 2).astype(f32)
        )

    both = jnp.concatenate(tables, 1)

    def back_to_tokens(parts):
        summed = jnp.einsum(
            "bct,bcd->btd", both, jnp.concatenate(parts, 1), preferred_element_type=f32
        ).astype(low)
        summed = summed.reshape(n_exp, 2, rows, width)
        mine = add_low(summed[:, 0], swap_on(summed[:, 1], "ctx", 1))
        return own_half_first(line_scatter([mine[(-o) % n_exp] for o in range(n_exp)], "exp"))

    sent_grads = back_to_tokens(sent)
    gate_parts = lax.all_gather(jnp.stack(gate_grad_parts, 1), ("ctx", "exp"), axis=0).reshape(
        n_ctx, n_exp, len(order), 2, rows
    )
    expert_ids = jnp.arange(expert_count, dtype=jnp.int32)
    gate_grads = jnp.zeros((rows, expert_count), f32)
    for at, (s, j) in enumerate(order):
        owner = (exp + s) % n_exp
        piece = pick(pick(gate_parts, ctx ^ j), owner)[at]
        there_core = core ^ j
        for i, first in enumerate((1 - grp, grp)):
            expert = owner * local_experts + 2 * there_core + first
            gate_grads = gate_grads + jnp.where(expert_ids[None, :] == expert, piece[i][:, None], 0.0)

    weighted = jnp.sum(gate_grads * gates, axis=1, keepdims=True)
    prob_grads = jnp.where(hits, (gate_grads - weighted) / sel_total, 0.0)
    logit_grads = probs * (prob_grads - jnp.sum(probs * prob_grads, axis=1, keepdims=True))
    router_float = router_weight.astype(f32)
    ffn_grads = sent_grads + jnp.dot(logit_grads, router_float.T, precision=lax.Precision.HIGHEST)
    router_grads = jnp.dot(ffn_low.astype(f32).T, logit_grads, precision=lax.Precision.HIGHEST)
    middle_grad = out_grad[0].astype(f32) + norm_backward(ffn_grads, middle_unit, middle_scale, gain_ffn)

    branch_grad = gather_ctx(by_exp(middle_grad.astype(low))).reshape(length, width)
    heads_grad = dot(branch_grad, weight_out).astype(low)
    joined_grads, gain_grads = attend_back(
        qkv, cosine, sine, doc_start, gains, attended, heads_grad, log_mass, heads
    )
    part_out = dot_tn(branch_grad, attended).astype(low)
    part_in = dot_tn(normed_seq, joined_grads).astype(low)
    normed_parts = dot_nt(joined_grads, weight_in).astype(low).reshape(n_ctx, rows, width)
    normed_grads = by_ctx(scatter_ctx(normed_parts))
    input_part = norm_backward(normed_grads, hidden_unit, hidden_scale, gain_attn)
    input_grad = (middle_grad + input_part).astype(low)[None]

    mixture = back_to_tokens(mixed)
    output = (middle + mixture).astype(low)[None]

    kept = add_low(grad_halves[1], swap_on(grad_halves[0].astype(low), "grp", 1)).reshape(2, quarter, -1)
    mine = pick(kept, core)
    sibling = swap_on(pick(kept, 1 - core), "ctx", 1)
    mine_x, sibling_x = swap_on(mine, "grp", 1), swap_on(sibling, "grp", 1)
    totals = []
    for at in range(local_experts):
        same_core = at // 2 == core
        same_grp = at % 2 == grp
        totals.append(
            jnp.where(
                same_core, jnp.where(same_grp, mine, mine_x), jnp.where(same_grp, sibling, sibling_x)
            ).astype(f32)
        )
    total = jnp.stack(totals, 1)
    expert_in_grad = total[:, :, : 2 * hidden_units].reshape(expert_in.shape)
    expert_out_grad = total[:, :, 2 * hidden_units :]

    def to_rows(part):
        blocks = part.reshape(n_exp, n_ctx * shard, part.shape[1])
        own = line_scatter([pick(blocks, (exp + o) % n_exp) for o in range(n_exp)], "exp")
        own = own.astype(low).reshape(n_ctx, shard, part.shape[1])
        pieces = [pick(own, ctx)] + [swap_on(pick(own, ctx ^ m), "ctx", m) for m in range(1, n_ctx)]
        placed = place_ctx(pieces)
        return placed.astype(f32) + swap_on(placed, "grp", 1).astype(f32)

    rows_out = to_rows(part_out)
    rows_in = to_rows(part_in)
    attn_out_grad = rows_out.transpose(1, 0, 2).reshape(shard, query_width)
    wide = heads * head_dim
    attn_in_grad = jnp.concatenate(
        [
            rows_in[:, :, :wide].transpose(1, 0, 2).reshape(shard, query_width),
            rows_in[:, :, wide : wide + head_dim].transpose(1, 0, 2).reshape(shard, kv_width),
            rows_in[:, :, wide + head_dim :].transpose(1, 0, 2).reshape(shard, kv_width),
        ],
        1,
    )

    norm_gain_grads = jnp.stack(
        [jnp.sum(normed_grads * hidden_unit, axis=0), jnp.sum(ffn_grads * middle_unit, axis=0)], axis=1
    )
    norm_total, head_total, router_total = lax.psum(
        (norm_gain_grads, gain_grads[:2].T, router_grads), ("grp", "ctx", "exp")
    )
    return (
        output,
        input_grad,
        attn_in_grad,
        attn_out_grad,
        norm_total,
        head_total,
        router_total,
        expert_in_grad,
        expert_out_grad,
    )


def solution(mesh):
    placed = (
        P(("grp", "exp"), "ctx", None),
        P(("grp", "exp"), "ctx", None),
        P(("grp", "exp"), None),
        P(("grp", "exp"), "ctx", None),
        P(("ctx", "exp"), None),
        P(("ctx", "exp"), None),
        P(),
        P(),
        P(),
        P("ctx", "exp", None, None),
        P("ctx", "exp", None),
    )
    sizes = dict(mesh.shape)
    body = per_device if sizes == {"grp": 2, "ctx": 4, "exp": 4} else per_device_general
    return jax.shard_map(
        body,
        mesh=mesh,
        in_specs=placed,
        out_specs=(
            P(("grp", "exp"), "ctx", None),
            P(("grp", "exp"), "ctx", None),
            P(("ctx", "exp"), None),
            P(("ctx", "exp"), None),
            P(),
            P(),
            P(),
            P("ctx", "exp", None, None),
            P("ctx", "exp", None),
        ),
        check_vma=False,
    )
```

```python
import functools

import jax
import jax.numpy as jnp
from jax import lax
from jax.experimental import pallas as pl
from jax.experimental.pallas import tpu as pltpu
from jax.sharding import PartitionSpec as P

epsilon = 1e-06
rotary_base = 1000000.0
key_span = 512


def doc_tables(lengths, positions):
    doc_ends = jnp.cumsum(lengths)
    passed = positions[:, None] >= doc_ends[None, :]
    doc_index = jnp.sum(passed.astype(jnp.int32), axis=1)
    first_pos = jnp.sum(jnp.where(passed, lengths[None, :], 0), axis=1)
    return (doc_index, positions - first_pos)


def rotate(values, relative, sign):
    half_dim = values.shape[-1] // 2
    freqs = rotary_base ** (-2.0 * jnp.arange(half_dim, dtype=jnp.float32) / values.shape[-1])
    angles = relative.astype(jnp.float32)[:, None] * freqs[None, :]
    cosine = jnp.cos(angles)[:, None, :]
    sine = sign * jnp.sin(angles)[:, None, :]
    first = values[..., :half_dim]
    second = values[..., half_dim:]
    return jnp.concatenate(
        [first * cosine - second * sine, second * cosine + first * sine], axis=-1
    )


def norm_forward(values, gain_vec):
    scale_vec = lax.rsqrt(jnp.mean(values * values, axis=-1, keepdims=True) + epsilon)
    unit_vec = values * scale_vec
    return (unit_vec * gain_vec, unit_vec, scale_vec)


def norm_backward(upstream, unit_vec, scale_vec, gain_vec):
    along = upstream * gain_vec
    return scale_vec * (along - unit_vec * jnp.mean(along * unit_vec, axis=-1, keepdims=True))


def per_device_general(
    hidden_in,
    out_grad,
    doc_lengths,
    routes,
    attention_input_weight,
    attn_out_weight,
    norm_gains,
    head_gains,
    router_weight,
    expert_in,
    expert_out,
):
    hidden = hidden_in[0].astype(jnp.float32)
    tokens_here, model_width = hidden.shape
    head_dim = head_gains.shape[0]
    expert_count = router_weight.shape[1]
    local_experts = expert_in.shape[1]
    route_picks = routes.shape[2]
    cycle_size = lax.axis_size("ctx")
    cycle_place = lax.axis_index("ctx")
    seq_length = tokens_here * cycle_size
    lengths = doc_lengths[0]
    query_pos = cycle_place * tokens_here + jnp.arange(tokens_here, dtype=jnp.int32)
    query_doc, query_rel = doc_tables(lengths, query_pos)
    gain_attn = norm_gains[:, 0].astype(jnp.float32)
    gain_ffn = norm_gains[:, 1].astype(jnp.float32)
    gain_query = head_gains[:, 0].astype(jnp.float32)
    gain_key = head_gains[:, 1].astype(jnp.float32)
    normed, hidden_unit, hidden_scale = norm_forward(hidden, gain_attn)
    normed_low = normed.astype(jnp.bfloat16)
    weight_in, weight_out = (
        lax.all_gather(attention_input_weight, ("ctx", "exp"), axis=0, tiled=True),
        lax.all_gather(attn_out_weight, ("ctx", "exp"), axis=0, tiled=True),
    )
    joined_projection = jnp.dot(normed_low, weight_in, preferred_element_type=jnp.float32)
    joined_width = weight_in.shape[1]
    query_width = weight_out.shape[1]
    head_count = query_width // head_dim
    kv_width = (joined_width - query_width) // 2
    kv_heads = kv_width // head_dim
    query_group_size = head_count // kv_heads
    query_raw = joined_projection[:, :query_width].reshape(tokens_here, head_count, head_dim)
    key_raw = joined_projection[:, query_width : query_width + kv_width].reshape(
        tokens_here, kv_heads, head_dim
    )
    value_low = joined_projection[:, query_width + kv_width :].astype(jnp.bfloat16)
    query_normed, query_unit, query_scale = norm_forward(query_raw, gain_query)
    key_normed, key_unit, key_scale = norm_forward(key_raw, gain_key)
    query_low = rotate(query_normed, query_rel, 1.0).astype(jnp.bfloat16)
    key_low = rotate(key_normed, query_rel, 1.0).astype(jnp.bfloat16)
    keys_local = jnp.stack([key_low.reshape(tokens_here, kv_width), value_low], axis=1)
    keys_all, in_all, out_all = (
        lax.all_gather(keys_local, "ctx", axis=0, tiled=True),
        lax.all_gather(expert_in, "ctx", axis=0, tiled=True),
        lax.all_gather(expert_out, "ctx", axis=0, tiled=True),
    )
    span = min(key_span, seq_length)
    block_count = seq_length // span
    key_blocks = keys_all.reshape(block_count, span, 2, kv_heads, head_dim)
    block_ids = jnp.arange(block_count, dtype=jnp.int32)
    query_rows = (
        query_low.reshape(tokens_here, kv_heads, query_group_size, head_dim)
        .transpose(1, 2, 0, 3)
        .reshape(kv_heads, query_group_size * tokens_here, head_dim)
    )
    score_scale = head_dim ** (-0.5)

    def block_scores(block_id, key_block):
        raw_scores = (
            jnp.einsum(
                "hrd,khd->hrk", query_rows, key_block[:, 0], preferred_element_type=jnp.float32
            )
            * score_scale
        )
        key_pos = block_id * span + jnp.arange(span, dtype=jnp.int32)
        key_doc = doc_tables(lengths, key_pos)[0]
        allowed = (key_pos[None, :] <= query_pos[:, None]) & (
            key_doc[None, :] == query_doc[:, None]
        )
        allowed = jnp.tile(allowed, (query_group_size, 1))[None]
        return (jnp.where(allowed, raw_scores, -1e30), allowed)

    def stats_step(running, scan_item):
        best_score, mass_sum = running
        block_id, key_block = scan_item
        masked, allowed = block_scores(block_id, key_block)
        new_best = jnp.maximum(best_score, jnp.max(masked, axis=-1))
        fresh = jnp.sum(jnp.where(allowed, jnp.exp(masked - new_best[..., None]), 0.0), axis=-1)
        return ((new_best, mass_sum * jnp.exp(best_score - new_best) + fresh), None)

    start_best = jnp.full((kv_heads, query_group_size * tokens_here), -1e30, jnp.float32)
    (best_score, mass_sum), unused = lax.scan(
        stats_step, (start_best, jnp.zeros_like(start_best)), (block_ids, key_blocks)
    )
    log_total = best_score + jnp.log(mass_sum)

    def value_step(summed, scan_item):
        block_id, key_block = scan_item
        masked, allowed = block_scores(block_id, key_block)
        weights = jnp.where(allowed, jnp.exp(masked - log_total[..., None]), 0.0).astype(
            jnp.bfloat16
        )
        return (
            summed
            + jnp.einsum(
                "hrk,khd->hrd", weights, key_block[:, 1], preferred_element_type=jnp.float32
            ),
            None,
        )

    start_rows = jnp.zeros((kv_heads, query_group_size * tokens_here, head_dim), jnp.float32)
    attended, unused = lax.scan(value_step, start_rows, (block_ids, key_blocks))
    attended_low = (
        attended.reshape(kv_heads, query_group_size, tokens_here, head_dim)
        .transpose(2, 0, 1, 3)
        .reshape(tokens_here, query_width)
        .astype(jnp.bfloat16)
    )
    branch = jnp.einsum("rc,dc->rd", attended_low, weight_out, preferred_element_type=jnp.float32)
    middle = hidden + branch
    ffn_normed, middle_unit, middle_scale = norm_forward(middle, gain_ffn)
    ffn_low = ffn_normed.astype(jnp.bfloat16)
    logits = jnp.dot(ffn_low, router_weight, preferred_element_type=jnp.float32)
    probs = jax.nn.softmax(logits, axis=-1)
    route_here = routes[0]
    route_hits = (
        route_here[:, :, None] == jnp.arange(expert_count, dtype=jnp.int32)[None, None, :]
    ).astype(jnp.float32)
    selected = jnp.sum(route_hits * probs[:, None, :], axis=-1)
    sel_total = jnp.sum(selected, axis=1, keepdims=True)
    gates = selected / sel_total
    capacity = 5 * tokens_here * route_picks // (4 * expert_count)
    flat_route = route_here.reshape(-1)
    slot_hits = (flat_route[:, None] == jnp.arange(expert_count, dtype=jnp.int32)[None, :]).astype(
        jnp.int32
    )
    slot_index = jnp.sum((jnp.cumsum(slot_hits, axis=0) - slot_hits) * slot_hits, axis=1)
    target = flat_route * capacity + slot_index
    exp_size = lax.axis_size("exp")
    buffer_shape = (exp_size, local_experts * capacity, model_width)
    arrive_shape = (exp_size, local_experts, capacity, model_width)
    empty_buffer = jnp.zeros((expert_count * capacity, model_width), jnp.bfloat16)
    outgoing = empty_buffer.at[target].set(jnp.repeat(ffn_low, route_picks, axis=0))
    arrived = lax.all_to_all(
        outgoing.reshape(buffer_shape), "exp", split_axis=0, concat_axis=0, tiled=True
    ).reshape(arrive_shape)
    gate_up = jnp.einsum("secd,dekf->seckf", arrived, in_all, preferred_element_type=jnp.float32)
    gate_part = gate_up[:, :, :, 0]
    up_part = gate_up[:, :, :, 1]
    sigmoid_part = jax.nn.sigmoid(gate_part)
    silu_part = jax.nn.silu(gate_part)
    act_low = (silu_part * up_part).astype(jnp.bfloat16)
    made = jnp.einsum(
        "secf,def->secd", act_low, out_all, preferred_element_type=jnp.float32
    ).astype(jnp.bfloat16)
    returned = lax.all_to_all(
        made.reshape(buffer_shape), "exp", split_axis=0, concat_axis=0, tiled=True
    ).reshape(expert_count * capacity, model_width)
    route_out = returned[target].astype(jnp.float32).reshape(tokens_here, route_picks, model_width)
    mixture = jnp.sum(gates[:, :, None] * route_out, axis=1)
    output = (middle + mixture).astype(jnp.bfloat16)[None]
    upstream = out_grad[0].astype(jnp.float32)
    gate_grads = jnp.sum(upstream[:, None, :] * route_out, axis=-1)
    route_grads = (
        (gates[:, :, None] * upstream[:, None, :])
        .astype(jnp.bfloat16)
        .reshape(tokens_here * route_picks, model_width)
    )
    outgoing_grads = empty_buffer.at[target].set(route_grads)
    grads_arrived = lax.all_to_all(
        outgoing_grads.reshape(buffer_shape), "exp", split_axis=0, concat_axis=0, tiled=True
    ).reshape(arrive_shape)
    act_grads = jnp.einsum(
        "secd,def->secf", grads_arrived, out_all, preferred_element_type=jnp.float32
    )
    gate_grad_part = act_grads * up_part * sigmoid_part * (1.0 + gate_part * (1.0 - sigmoid_part))
    gate_up_grads = jnp.stack([gate_grad_part, act_grads * silu_part], axis=3).astype(jnp.bfloat16)
    input_rows = jnp.einsum(
        "seckf,dekf->secd", gate_up_grads, in_all, preferred_element_type=jnp.float32
    ).astype(jnp.bfloat16)
    came_back = lax.all_to_all(
        input_rows.reshape(buffer_shape), "exp", split_axis=0, concat_axis=0, tiled=True
    ).reshape(expert_count * capacity, model_width)
    sent_grads = jnp.sum(
        came_back[target].astype(jnp.float32).reshape(tokens_here, route_picks, model_width), axis=1
    )
    term_in = jnp.einsum(
        "secd,seckf->dekf", arrived, gate_up_grads, preferred_element_type=jnp.float32
    )
    term_out = jnp.einsum(
        "secd,secf->def", grads_arrived, act_low, preferred_element_type=jnp.float32
    )
    expert_local = lax.psum_scatter(
        jnp.concatenate([term_in, term_out[:, :, None, :]], axis=2).astype(jnp.bfloat16),
        "ctx",
        scatter_dimension=0,
        tiled=True,
    )
    weighted = jnp.sum(gate_grads * gates, axis=1, keepdims=True)
    sel_grads = (gate_grads - weighted) / sel_total
    prob_grads = jnp.sum(sel_grads[:, :, None] * route_hits, axis=1)
    logit_grads = probs * (prob_grads - jnp.sum(probs * prob_grads, axis=1, keepdims=True))
    router_float = router_weight.astype(jnp.float32)
    ffn_grads = sent_grads + jnp.dot(logit_grads, router_float.T, precision=lax.Precision.HIGHEST)
    router_grads = jnp.dot(
        ffn_low.astype(jnp.float32).T, logit_grads, precision=lax.Precision.HIGHEST
    )
    middle_grad = upstream + norm_backward(ffn_grads, middle_unit, middle_scale, gain_ffn)
    attn_grad_low = middle_grad.astype(jnp.bfloat16)
    heads_grad_low = jnp.dot(attn_grad_low, weight_out, preferred_element_type=jnp.float32).astype(
        jnp.bfloat16
    )
    grad_rows = (
        heads_grad_low.reshape(tokens_here, kv_heads, query_group_size, head_dim)
        .transpose(1, 2, 0, 3)
        .reshape(kv_heads, query_group_size * tokens_here, head_dim)
    )

    def delta_step(summed, scan_item):
        block_id, key_block = scan_item
        masked, allowed = block_scores(block_id, key_block)
        weights = jnp.where(allowed, jnp.exp(masked - log_total[..., None]), 0.0)
        weight_grads = jnp.einsum(
            "hrd,khd->hrk", grad_rows, key_block[:, 1], preferred_element_type=jnp.float32
        )
        return (summed + jnp.sum(weights * weight_grads, axis=-1), None)

    delta_sum, unused = lax.scan(delta_step, jnp.zeros_like(log_total), (block_ids, key_blocks))

    def grad_step(query_grads, scan_item):
        block_id, key_block = scan_item
        masked, allowed = block_scores(block_id, key_block)
        weights = jnp.where(allowed, jnp.exp(masked - log_total[..., None]), 0.0)
        weight_grads = jnp.einsum(
            "hrd,khd->hrk", grad_rows, key_block[:, 1], preferred_element_type=jnp.float32
        )
        score_grads = (weights * (weight_grads - delta_sum[..., None])).astype(jnp.bfloat16)
        query_grads = (
            query_grads
            + jnp.einsum(
                "hrk,khd->hrd", score_grads, key_block[:, 0], preferred_element_type=jnp.float32
            )
            * score_scale
        )
        key_grads = (
            jnp.einsum("hrk,hrd->khd", score_grads, query_rows, preferred_element_type=jnp.float32)
            * score_scale
        )
        value_grads = jnp.einsum(
            "hrk,hrd->khd",
            weights.astype(jnp.bfloat16),
            grad_rows,
            preferred_element_type=jnp.float32,
        )
        return (query_grads, jnp.stack([key_grads, value_grads], axis=1))

    query_grads, block_grads = lax.scan(grad_step, start_rows, (block_ids, key_blocks))
    key_value_grads = lax.psum_scatter(
        block_grads.reshape(seq_length, 2, kv_width).astype(jnp.bfloat16),
        "ctx",
        scatter_dimension=0,
        tiled=True,
    ).astype(jnp.float32)
    query_grads = (
        query_grads.reshape(kv_heads, query_group_size, tokens_here, head_dim)
        .transpose(2, 0, 1, 3)
        .reshape(tokens_here, head_count, head_dim)
    )
    query_turned = rotate(query_grads, query_rel, -1.0)
    query_proj = norm_backward(query_turned, query_unit, query_scale, gain_query)
    key_turned = rotate(
        key_value_grads[:, 0].reshape(tokens_here, kv_heads, head_dim), query_rel, -1.0
    )
    key_proj = norm_backward(key_turned, key_unit, key_scale, gain_key)
    head_gain_grads = jnp.stack(
        [
            jnp.sum(query_turned * query_unit, axis=(0, 1)),
            jnp.sum(key_turned * key_unit, axis=(0, 1)),
        ],
        axis=1,
    )
    joined_grads = jnp.concatenate(
        [
            query_proj.reshape(tokens_here, query_width),
            key_proj.reshape(tokens_here, kv_width),
            key_value_grads[:, 1],
        ],
        axis=1,
    ).astype(jnp.bfloat16)
    normed_grads = jnp.einsum(
        "rc,dc->rd", joined_grads, weight_in, preferred_element_type=jnp.float32
    )
    input_part = norm_backward(normed_grads, hidden_unit, hidden_scale, gain_attn)
    input_grad = (middle_grad + input_part).astype(jnp.bfloat16)[None]
    norm_gain_grads = jnp.stack(
        [jnp.sum(normed_grads * hidden_unit, axis=0), jnp.sum(ffn_grads * middle_unit, axis=0)],
        axis=1,
    )
    norm_total, head_total, router_total = lax.psum(
        (norm_gain_grads, head_gain_grads, router_grads), ("grp", "ctx", "exp")
    )
    part_in = jnp.einsum("rc,rq->cq", normed_low, joined_grads, preferred_element_type=jnp.float32)
    part_out = jnp.einsum(
        "rc,rq->cq", attn_grad_low, attended_low, preferred_element_type=jnp.float32
    )
    dense_local = lax.psum_scatter(
        jnp.concatenate([part_in, part_out], axis=1),
        ("ctx", "exp"),
        scatter_dimension=0,
        tiled=True,
    )
    dense_total, expert_total = (
        lax.psum(dense_local.astype(jnp.bfloat16), "grp").astype(jnp.float32),
        lax.psum(expert_local, "grp").astype(jnp.float32),
    )
    return (
        output,
        input_grad,
        dense_total[:, :joined_width],
        dense_total[:, joined_width:],
        norm_total,
        head_total,
        router_total,
        expert_total[:, :, :2],
        expert_total[:, :, 2],
    )


NT = (((1,), (1,)), ((), ()))

def head_norm(raw):
    scale = lax.rsqrt(jnp.mean(raw * raw, axis=-1, keepdims=True) + epsilon)
    return raw * scale, scale

def turn(values, cosine, sine):
    return values * cosine + pltpu.roll(values, values.shape[-1] // 2, 1) * sine

def dots(a, b):
    return jnp.dot(a, b, preferred_element_type=jnp.float32)

def dots_nt(a, b):
    return lax.dot_general(a, b, NT, preferred_element_type=jnp.float32)

def allowed_chunk(start, i, j, tile):
    key_pos = j * tile + lax.broadcasted_iota(jnp.int32, (tile, tile), 0)
    ok = key_pos >= start
    if i == j:
        query_pos = i * tile + lax.broadcasted_iota(jnp.int32, (tile, tile), 1)
        ok = ok & (key_pos <= query_pos)
    return ok

def attend_kernel(tile, q_ref, k_ref, v_ref, cos_ref, sin_ref, start_ref, gain_ref,
                  o_ref, lse_ref, key_s, value_t):
    length, head_dim = q_ref.shape
    c = head_dim ** -0.5 * 1.4426950408889634
    @pl.when(pl.program_id(0) == 0)
    def _():
        unit, _ = head_norm(k_ref[...])
        key_s[...] = turn(unit * gain_ref[1:2], cos_ref[...], sin_ref[...]).astype(jnp.bfloat16)
        value_t[...] = v_ref[...].T.astype(jnp.bfloat16)
    unit, _ = head_norm(q_ref[...])
    query = turn(unit * gain_ref[0:1], cos_ref[...], sin_ref[...]).astype(jnp.bfloat16)
    for i in range(length // tile):
        rows = slice(i * tile, (i + 1) * tile)
        start = start_ref[:, rows]
        mass = jnp.zeros((1, tile), jnp.float32)
        total = jnp.zeros((head_dim, tile), jnp.float32)
        for j in range(i + 1):
            cols = slice(j * tile, (j + 1) * tile)
            s = dots_nt(key_s[cols, :], query[rows])
            p = jnp.where(allowed_chunk(start, i, j, tile), jnp.exp2(s * c), 0.0)
            mass = mass + jnp.sum(p, axis=0, keepdims=True)
            total = total + dots(value_t[:, cols], p.astype(jnp.bfloat16))
        o_ref[rows, :] = (total / mass).T.astype(jnp.bfloat16)
        lse_ref[0, :, rows] = jnp.log2(mass)

def attend(qkv, cosine, sine, start, gains, heads):
    length, head_dim = cosine.shape
    full = lambda shape: pl.BlockSpec(shape, lambda h: (0, 0))
    col = lambda at: pl.BlockSpec((length, head_dim), lambda h: (0, at))
    return pl.pallas_call(
        functools.partial(attend_kernel, min(256, length)),
        grid=(heads,),
        in_specs=[
            pl.BlockSpec((length, head_dim), lambda h: (0, h)), col(heads), col(heads + 1),
            full((length, head_dim)), full((length, head_dim)), full((1, length)), full(gains.shape),
        ],
        out_specs=[
            pl.BlockSpec((length, head_dim), lambda h: (0, h)),
            pl.BlockSpec((1, 1, length), lambda h: (h, 0, 0)),
        ],
        out_shape=[
            jax.ShapeDtypeStruct((length, heads * head_dim), jnp.bfloat16),
            jax.ShapeDtypeStruct((heads, 1, length), jnp.float32),
        ],
        scratch_shapes=[
            pltpu.VMEM((length, head_dim), jnp.bfloat16),
            pltpu.VMEM((head_dim, length), jnp.bfloat16),
        ],
        compiler_params=pltpu.CompilerParams(vmem_limit_bytes=48 * 2**20),
    )(qkv, qkv, qkv, cosine, sine, start, gains)

def attend_back_kernel(tile, heads, q_ref, k_ref, v_ref, cos_ref, sin_ref, start_ref, gain_ref,
                       o_ref, go_ref, lse_ref, grad_ref, gain_grad_ref,
                       key_s, key_t, value_s, key_grad, value_grad, query_grad):
    length, head_dim = q_ref.shape
    scale = head_dim ** -0.5
    c = scale * 1.4426950408889634
    step = pl.program_id(0)

    def norm_back(turned_grad, raw, row):
        back = turn(turned_grad, cos_ref[...], -sin_ref[...])
        unit, unit_scale = head_norm(raw)
        gain_grad_ref[row:row + 1] += jnp.sum(back * unit, axis=0, keepdims=True)
        along = back * gain_ref[row:row + 1]
        return unit_scale * (along - unit * jnp.mean(along * unit, axis=-1, keepdims=True))

    @pl.when(step == 0)
    def _():
        unit, _ = head_norm(k_ref[...])
        key = turn(unit * gain_ref[1:2], cos_ref[...], sin_ref[...])
        key_s[...] = key.astype(jnp.bfloat16)
        key_t[...] = key.T.astype(jnp.bfloat16)
        value_s[...] = v_ref[...].astype(jnp.bfloat16)
        key_grad[...] = jnp.zeros_like(key_grad)
        value_grad[...] = jnp.zeros_like(value_grad)
        gain_grad_ref[...] = jnp.zeros_like(gain_grad_ref)

    @pl.when(step < heads)
    def _():
        unit, _ = head_norm(q_ref[...])
        query = turn(unit * gain_ref[0:1], cos_ref[...], sin_ref[...]).astype(jnp.bfloat16)
        for i in range(length // tile):
            rows = slice(i * tile, (i + 1) * tile)
            start = start_ref[:, rows]
            lse = lse_ref[0, :, rows]
            up = go_ref[rows, :]
            delta = jnp.sum((up.astype(jnp.float32) * o_ref[rows, :].astype(jnp.float32)).T, axis=0, keepdims=True)
            q_i = query[rows]
            total = jnp.zeros((head_dim, tile), jnp.float32)
            for j in range(i + 1):
                cols = slice(j * tile, (j + 1) * tile)
                s = dots_nt(key_s[cols, :], q_i)
                p = jnp.where(allowed_chunk(start, i, j, tile), jnp.exp2(s * c - lse), 0.0)
                dp = dots_nt(value_s[cols, :], up)
                ds = (p * (dp - delta)).astype(jnp.bfloat16)
                value_grad[cols, :] += dots(p.astype(jnp.bfloat16), up)
                key_grad[cols, :] += dots(ds, q_i)
                total = total + dots(key_t[:, cols], ds)
            query_grad[rows, :] = (total * scale).T
        grad_ref[...] = norm_back(query_grad[...], q_ref[...], 0).astype(jnp.bfloat16)

    @pl.when(step == heads)
    def _():
        grad_ref[...] = norm_back(key_grad[...] * scale, k_ref[...], 1).astype(jnp.bfloat16)

    @pl.when(step == heads + 1)
    def _():
        grad_ref[...] = value_grad[...].astype(jnp.bfloat16)

def attend_back(qkv, cosine, sine, start, gains, attended, upstream, lse, heads):
    length, head_dim = cosine.shape
    full = lambda shape: pl.BlockSpec(shape, lambda h: (0, 0))
    col = lambda at: pl.BlockSpec((length, head_dim), lambda h: (0, at))
    per_head = pl.BlockSpec((length, head_dim), lambda h: (0, jnp.minimum(h, heads - 1)))
    return pl.pallas_call(
        functools.partial(attend_back_kernel, min(256, length), heads),
        grid=(heads + 2,),
        in_specs=[
            per_head, col(heads), col(heads + 1),
            full((length, head_dim)), full((length, head_dim)), full((1, length)), full(gains.shape),
            per_head, per_head,
            pl.BlockSpec((1, 1, length), lambda h: (jnp.minimum(h, heads - 1), 0, 0)),
        ],
        out_specs=[
            pl.BlockSpec((length, head_dim), lambda h: (0, h)),
            full((8, head_dim)),
        ],
        out_shape=[
            jax.ShapeDtypeStruct((length, (heads + 2) * head_dim), jnp.bfloat16),
            jax.ShapeDtypeStruct((8, head_dim), jnp.float32),
        ],
        scratch_shapes=[
            pltpu.VMEM((length, head_dim), jnp.bfloat16),
            pltpu.VMEM((head_dim, length), jnp.bfloat16),
            pltpu.VMEM((length, head_dim), jnp.bfloat16),
            pltpu.VMEM((length, head_dim), jnp.float32),
            pltpu.VMEM((length, head_dim), jnp.float32),
            pltpu.VMEM((length, head_dim), jnp.float32),
        ],
        compiler_params=pltpu.CompilerParams(vmem_limit_bytes=48 * 2**20),
    )(qkv, qkv, qkv, cosine, sine, start, gains, attended, upstream, lse)


def expert_kernel(blocks, capacity, piece_count, *refs):
    tok0, tok1, up0, up1, router_ref = refs[:5]
    weights = refs[5 : 5 + 6 * piece_count]
    x_out, up_out, gug_out, act_out, sent0, sent1, mix0, mix1 = refs[-18:-10]
    x_s, up_s, table_s, gate_s, y_acc, sent_acc, gg_acc, gate_tab0, gate_tab1, gg_rows = refs[-10:]
    tokens, ups = (tok0, tok1), (up0, up1)
    rows = tok0.shape[0]
    span = tok0.shape[1] // piece_count
    half = capacity
    ctx, grp, exp = lax.axis_index("ctx"), lax.axis_index("grp"), lax.axis_index("exp")
    core = ctx % 2
    step_e, step_f = pl.program_id(0), pl.program_id(1)
    experts = router_ref.shape[0]
    expert = exp * 4 + 2 * core + jnp.where(step_e == 0, 1 - grp, grp)
    order = [pl.ds(pl.multiple_of((q ^ core) * span, span), span) for q in range(piece_count)]

    @pl.when((step_e == 0) & (step_f == 0))
    def _():
        gg_rows[...] = jnp.zeros_like(gg_rows)
        for kk, tab in enumerate((gate_tab0, gate_tab1)):
            logits = dots_nt(router_ref[...], tokens[kk][...])
            powers = jnp.exp(logits - jnp.max(logits, axis=0, keepdims=True))
            probs = powers / jnp.sum(powers, axis=0, keepdims=True)
            slot = ups[kk][rows:, :rows].astype(jnp.float32)
            chosen = jnp.where(slot >= 0, probs, 0.0)
            tab[...] = chosen / jnp.sum(chosen, axis=0, keepdims=True)

    @pl.when(step_f == 0)
    def _():
        y_acc[...] = jnp.zeros_like(y_acc)
        sent_acc[...] = jnp.zeros_like(sent_acc)
        gg_acc[...] = jnp.zeros_like(gg_acc)
        which = lax.broadcasted_iota(jnp.int32, (experts, rows), 0) == expert
        for kk, tab in enumerate((gate_tab0, gate_tab1)):
            slots = ups[kk][rows:, :rows].astype(jnp.float32)
            slot = jnp.sum(jnp.where(which, slots, 0.0), axis=0, keepdims=True)
            gate = jnp.sum(jnp.where(which, tab[...], 0.0), axis=0, keepdims=True)
            table = slot == lax.broadcasted_iota(jnp.int32, (capacity, rows), 0).astype(jnp.float32)
            table_low = jnp.where(table, 1.0, 0.0).astype(jnp.bfloat16)
            table_s[kk] = table_low
            at = slice(kk * half, (kk + 1) * half)
            gate_s[at, :] = jnp.sum(jnp.where(table, gate, 0.0), axis=1, keepdims=True)
            for q in range(piece_count):
                cols = slice(q * span, (q + 1) * span)
                x_s[at, cols] = dots(table_low, tokens[kk][:, order[q]]).astype(jnp.bfloat16)
                up_s[at, cols] = dots(table_low, ups[kk][:rows, order[q]]).astype(jnp.bfloat16)
        x_out[0] = x_s[...]
        up_out[0] = up_s[...]

    def body(parts):
        gates, upw, outs = parts[0::3], parts[1::3], parts[2::3]
        wide = gates[0].shape[1]
        cut = [slice(q * span, (q + 1) * span) for q in range(piece_count)]
        a = sum(dots(x_s[:, cut[q]], gates[q][...]) for q in range(piece_count))
        u = sum(dots(x_s[:, cut[q]], upw[q][...]) for q in range(piece_count))
        back = sum(dots(up_s[:, cut[q]], outs[q][...]) for q in range(piece_count))
        s = 1.0 / (1.0 + jnp.exp(-a))
        silu = a * s
        act = (silu * u).astype(jnp.bfloat16).astype(jnp.float32)
        gg_acc[...] += jnp.sum(act * back, axis=1, keepdims=True)
        gate = gate_s[...]
        act_low = (act * gate).astype(jnp.bfloat16)
        back = back * gate
        gate_grad = (back * u * s * (1.0 + a * (1.0 - s))).astype(jnp.bfloat16)
        up_grad = (back * silu).astype(jnp.bfloat16)
        at = pl.multiple_of(step_f * wide, wide)
        total = gug_out.shape[2] // 2
        gug_out[0, :, pl.ds(at, wide)] = gate_grad
        gug_out[0, :, pl.ds(pl.multiple_of(total + at, wide), wide)] = up_grad
        act_out[0, :, pl.ds(at, wide)] = act_low
        for q in range(piece_count):
            y_acc[:, cut[q]] += dots_nt(act_low, outs[q][...])
            sent_acc[:, cut[q]] += dots_nt(gate_grad, gates[q][...]) + dots_nt(up_grad, upw[q][...])

    @pl.when(step_e == 0)
    def _():
        body(weights[: 3 * piece_count])

    @pl.when(step_e == 1)
    def _():
        body(weights[3 * piece_count :])

    def finish(first):
        which = lax.broadcasted_iota(jnp.int32, (experts, rows), 0) == expert
        for kk, (sent, mix) in enumerate(((sent0, mix0), (sent1, mix1))):
            table = table_s[kk]
            at = slice(kk * half, (kk + 1) * half)
            for q in range(piece_count):
                cols = slice(q * span, (q + 1) * span)
                for out, acc, size in ((sent, sent_acc, rows), (mix, y_acc, rows)):
                    part = lax.dot_general(
                        table, acc[at, cols].astype(jnp.bfloat16), (((0,), (0,)), ((), ())),
                        preferred_element_type=jnp.float32,
                    )
                    if not first:
                        part = part + out[:rows, order[q]].astype(jnp.float32)
                    out[:rows, order[q]] = part.astype(jnp.bfloat16)
            gg = jnp.sum(jnp.where(table > 0, gg_acc[at, :], 0.0), axis=0, keepdims=True)
            gg_rows[kk] += jnp.where(which, gg, 0.0)
            if not first:
                high = gg_rows[kk].astype(jnp.bfloat16)
                sent[rows:, :] = jnp.zeros((sent.shape[0] - rows, sent.shape[1]), jnp.bfloat16)
                sent[rows:, :rows] = high
                sent[rows:, rows : 2 * rows] = (gg_rows[kk] - high.astype(jnp.float32)).astype(jnp.bfloat16)

    last = pl.num_programs(1) - 1

    @pl.when((step_f == last) & (step_e == 0))
    def _():
        finish(True)

    @pl.when((step_f == last) & (step_e == 1))
    def _():
        finish(False)


def run_experts(block, blocks, tok, ups, router_t, pieces, capacity, held):
    rows, width = tok[0].shape
    count = len(pieces[0])
    quarter, wide3 = pieces[0][0].shape
    units = wide3 // 3
    tile = min(256, units)
    steps = units // tile
    cap2 = 2 * capacity
    low = jnp.bfloat16
    once = pl.Buffered(1)
    whole = lambda a: pl.BlockSpec(a.shape, lambda e, f: (0, 0), pipeline_mode=once)
    in_specs = [whole(a) for a in (*tok, *ups, router_t)]
    operands = [*tok, *ups, router_t]
    for j in range(2):
        for piece in pieces[j]:
            for part in range(3):
                def at(e, f, j=j, part=part):
                    return (0, part * steps + (jnp.where(e == 0, f, steps - 1) if j == 0 else jnp.where(e == 1, f, 0)))
                in_specs.append(pl.BlockSpec((quarter, tile), at))
                operands.append(piece)
    aliases = {}
    if held is not None:
        for i, a in enumerate(held):
            aliases[len(operands)] = i
            operands.append(a)
            in_specs.append(pl.BlockSpec(memory_space=pl.ANY))
    store = lambda cols: pl.BlockSpec((1, cap2, cols), lambda e, f: (e, block, 0))
    whole_out = lambda r: pl.BlockSpec((r, width), lambda e, f: (0, 0), pipeline_mode=once)
    ext = ups[0].shape[0]
    struct = jax.ShapeDtypeStruct
    experts = router_t.shape[0]

    def kernel(*refs):
        n_in = 5 + 6 * count
        held_n = 4 if held is not None else 0
        expert_kernel(blocks, capacity, count, *refs[:n_in], *refs[n_in + held_n :])

    return pl.pallas_call(
        kernel,
        grid=(2, steps),
        in_specs=in_specs,
        out_specs=[
            store(width), store(width), store(2 * units), store(units),
            whole_out(ext), whole_out(ext), whole_out(rows), whole_out(rows),
        ],
        out_shape=[
            struct((2, blocks * cap2, width), low), struct((2, blocks * cap2, width), low),
            struct((2, blocks * cap2, 2 * units), low), struct((2, blocks * cap2, units), low),
            struct((ext, width), low), struct((ext, width), low),
            struct((rows, width), low), struct((rows, width), low),
        ],
        scratch_shapes=[
            pltpu.VMEM((cap2, width), low), pltpu.VMEM((cap2, width), low),
            pltpu.VMEM((2, capacity, rows), low), pltpu.VMEM((cap2, 1), jnp.float32),
            pltpu.VMEM((cap2, width), jnp.float32), pltpu.VMEM((cap2, width), jnp.float32),
            pltpu.VMEM((cap2, 1), jnp.float32),
            pltpu.VMEM((experts, rows), jnp.float32), pltpu.VMEM((experts, rows), jnp.float32),
            pltpu.VMEM((2, experts, rows), jnp.float32),
        ],
        input_output_aliases=aliases,
        compiler_params=pltpu.CompilerParams(vmem_limit_bytes=60 * 2**20),
    )(*operands)


low = jnp.bfloat16


def swap_on(value, axis, mask):
    count = lax.axis_size(axis)
    return lax.ppermute(value, axis, [(i, i ^ mask) for i in range(count)])


def after(value, *others):
    return lax.optimization_barrier((value, *others))[0]


def line_chain(block, axis, then=None):
    n = lax.axis_size(axis)
    rights, lefts = [block], [block]
    for s in range(1, n):
        if s == 2 and then is not None:
            rights[1], lefts[1] = after(rights[1], then), after(lefts[1], then)
        rights.append(lax.ppermute(rights[-1], axis, [(i, i + 1) for i in range(s - 1, n - 1)]))
        lefts.append(lax.ppermute(lefts[-1], axis, [(i, i - 1) for i in range(1, n - s + 1)]))
    return rights, lefts


def shift_back(value, axis, s):
    n = lax.axis_size(axis)
    return lax.ppermute(value, axis, [(i, (i - s) % n) for i in range(n)])


def sum_all(value):
    for axis in ("grp", "ctx", "exp"):
        mask = 1
        while mask < lax.axis_size(axis):
            value = value + swap_on(value, axis, mask)
            mask *= 2
    return value


def add_low(a, b):
    return (a.astype(jnp.float32) + b.astype(jnp.float32)).astype(low)


def pick(array, index):
    return lax.dynamic_index_in_dim(array, index, 0, keepdims=False)


def per_device(
    hidden_in,
    out_grad,
    doc_lengths,
    routes,
    attention_input_weight,
    attn_out_weight,
    norm_gains,
    head_gains,
    router_weight,
    expert_in,
    expert_out,
):
    hidden = hidden_in[0].astype(jnp.float32)
    rows, width = hidden.shape
    head_dim = head_gains.shape[0]
    expert_count = router_weight.shape[1]
    top = routes.shape[2]
    n_ctx, n_exp = lax.axis_size("ctx"), lax.axis_size("exp")
    grp, ctx, exp = lax.axis_index("grp"), lax.axis_index("ctx"), lax.axis_index("exp")
    half, core = ctx // 2, ctx % 2
    length = rows * n_ctx
    query_width = attn_out_weight.shape[1]
    kv_width = (attention_input_weight.shape[1] - query_width) // 2
    heads = query_width // head_dim // n_ctx
    shard = attention_input_weight.shape[0]
    f32 = jnp.float32

    def dot(a, b):
        return jnp.dot(a, b, preferred_element_type=f32)

    def dot_nt(a, b):
        return lax.dot_general(a, b, (((1,), (1,)), ((), ())), preferred_element_type=f32)

    def dot_tn(a, b):
        return lax.dot_general(a, b, (((0,), (0,)), ((), ())), preferred_element_type=f32)

    def by_exp(a):
        return a.reshape(a.shape[0], n_ctx, n_exp, shard).transpose(0, 2, 1, 3).reshape(a.shape)

    def by_ctx(a):
        return a.reshape(a.shape[0], n_exp, n_ctx, shard).transpose(0, 2, 1, 3).reshape(a.shape)

    def own_half_first(a):
        return jnp.where(half == 0, a, jnp.concatenate([a[:, width // 2 :], a[:, : width // 2]], 1))

    def gather_ctx(block):
        over = swap_on(block, "ctx", 2)
        blocks = [block, swap_on(block, "ctx", 1), over, swap_on(over, "ctx", 1)]
        return place_ctx(blocks)

    def place_ctx(blocks):
        out = jnp.zeros((n_ctx,) + blocks[0].shape, blocks[0].dtype)
        for m in range(n_ctx):
            out = lax.dynamic_update_index_in_dim(out, blocks[m], ctx ^ m, 0)
        return out

    def scatter_ctx(parts):
        got = swap_on(jnp.stack([pick(parts, ctx ^ 1), pick(parts, ctx ^ 3)]), "ctx", 1)
        mine = pick(parts, ctx).astype(f32) + got[0].astype(f32)
        other = add_low(pick(parts, ctx ^ 2), got[1])
        return mine + swap_on(other, "ctx", 2).astype(f32)

    positions = jnp.arange(length, dtype=jnp.int32)
    relative = doc_tables(doc_lengths[0], positions)[1]
    doc_start = (positions - relative)[None, :]
    freqs = rotary_base ** (-2.0 * jnp.arange(head_dim // 2, dtype=f32) / head_dim)
    angles = relative.astype(f32)[:, None] * freqs[None, :]
    cosine = jnp.concatenate([jnp.cos(angles)] * 2, 1)
    sine = jnp.concatenate([-jnp.sin(angles), jnp.sin(angles)], 1)
    gains = jnp.pad(head_gains.astype(f32).T, ((0, 6), (0, 0)))
    gain_attn = norm_gains[:, 0].astype(f32)
    gain_ffn = norm_gains[:, 1].astype(f32)

    def weight_in_of(at):
        return jnp.concatenate(
            [
                lax.dynamic_slice_in_dim(attention_input_weight, at * heads * head_dim, heads * head_dim, 1),
                lax.dynamic_slice_in_dim(attention_input_weight, query_width + at * head_dim, head_dim, 1),
                lax.dynamic_slice_in_dim(
                    attention_input_weight, query_width + kv_width + at * head_dim, head_dim, 1
                ),
            ],
            1,
        )

    def weight_out_of(at):
        return lax.dynamic_slice_in_dim(attn_out_weight, at * heads * head_dim, heads * head_dim, 1)

    def to_ctx(piece_of, then=None):
        pieces = [piece_of(ctx ^ m) for m in range(n_ctx)]
        if then is not None:
            pieces = [after(p, then) for p in pieces]
        return place_ctx([pieces[0]] + [swap_on(pieces[m], "ctx", m) for m in range(1, n_ctx)])

    def all_rows(block, then=None):
        halves = block.reshape((2, n_ctx // 2) + block.shape[1:])
        half_block = pick(halves, grp)
        if then is not None:
            half_block = after(half_block, then)
        rights, lefts = line_chain(half_block, "exp")
        cross = lambda value, held: lax.ppermute(
            value, ("grp", "exp"), [(g * n_exp + i, (1 - g) * n_exp + i) for g in range(2) for i in held]
        )
        rights_x, lefts_x = [None], [None]
        for s in range(1, n_exp):
            rights_x.append(cross(rights[s], range(s, n_exp)))
            lefts_x.append(cross(lefts[s], range(n_exp - s)))
        out = jnp.zeros((n_exp,) + halves.shape, block.dtype)
        out = lax.dynamic_update_index_in_dim(out, halves, exp, 0)
        for s in range(1, n_exp):
            for which, r, l in ((grp, rights, lefts), (1 - grp, rights_x, lefts_x)):
                got = (r[s] + l[n_exp - s])[None, None]
                out = lax.dynamic_update_slice(out, got, ((exp - s) % n_exp, which, 0, 0, 0))
        return out.reshape(width, block.shape[-1]), rights[n_exp - 1]

    normed, hidden_unit, hidden_scale = norm_forward(hidden, gain_attn)
    normed_seq = gather_ctx(by_exp(normed.astype(low))).reshape(length, width)
    capacity = 5 * rows * top // (4 * expert_count)
    hits = jnp.any(routes[0][:, :, None] == jnp.arange(expert_count, dtype=jnp.int32), axis=1)
    before = jnp.tril(jnp.ones((rows, rows), low), -1)
    slots = jnp.where(hits, dot(before, hits.astype(low)), -1.0).T.astype(low)
    upstream_block = jnp.concatenate(
        [own_half_first(out_grad[0]), jnp.pad(slots, ((0, 0), (0, width - rows)))]
    )
    block_in = to_ctx(weight_in_of)
    block_out = to_ctx(weight_out_of, block_in)
    weight_in, in_done = all_rows(block_in)
    weight_out, out_done = all_rows(block_out, in_done)
    up_rights, up_lefts = line_chain(upstream_block, "exp", out_done)

    local_experts = expert_in.shape[1]
    hidden_units = expert_out.shape[2]
    quarter = expert_in.shape[0]

    def expert_rows(at):
        return jnp.concatenate(
            [
                lax.dynamic_index_in_dim(expert_in, at, 1, keepdims=False).reshape(quarter, -1),
                lax.dynamic_index_in_dim(expert_out, at, 1, keepdims=False),
            ],
            1,
        )

    here = [2 * core + (1 - grp), 2 * core + grp]
    there = [2 * (1 - core) + (1 - grp), 2 * (1 - core) + grp]
    over_same = swap_on(after(expert_rows(here[0]), block_out), "ctx", 2)
    over_other = swap_on(after(expert_rows(there[0]), block_out), "ctx", 3)
    expert_weights = []
    for j in range(2):
        same, other = expert_rows(here[j]), swap_on(expert_rows(there[j]), "ctx", 1)
        if j == 1:
            over_same, over_other = swap_on(over_same, "grp", 1), swap_on(over_other, "grp", 1)
        expert_weights.append([same, other, over_same, over_other])

    qkv = dot(normed_seq, weight_in)
    attended, log_mass = attend(qkv, cosine, sine, doc_start, gains, heads)
    branch = dot_nt(attended, weight_out).astype(low).reshape(n_ctx, rows, width)
    middle = hidden + by_ctx(scatter_ctx(branch))
    ffn_normed, middle_unit, middle_scale = norm_forward(middle, gain_ffn)
    ffn_low = ffn_normed.astype(low)

    logits = dot(ffn_low, router_weight)
    probs = jax.nn.softmax(logits, axis=-1)
    selected = jnp.where(hits, probs, 0.0)
    sel_total = jnp.sum(selected, axis=-1, keepdims=True)
    gates = selected / sel_total

    tok_rights, tok_lefts = line_chain(own_half_first(ffn_low), "exp")
    router_here = own_half_first(router_weight.T)
    held, backs, mixes = None, [], []
    for s in range(n_exp):
        if s == 0:
            tok, ups = tok_rights[0], up_rights[0]
        else:
            tok, ups = tok_rights[s] + tok_lefts[n_exp - s], up_rights[s] + up_lefts[n_exp - s]
        tok, ups = (tok, swap_on(tok, "ctx", 1)), (ups, swap_on(ups, "ctx", 1))
        *held, back0, back1, mix0, mix1 = run_experts(
            s, n_exp, tok, ups, router_here, expert_weights, capacity, held
        )
        back = add_low(back0, swap_on(back1, "ctx", 1))
        backs.append(back if s == 0 else shift_back(back, "exp", s))
        mixes.append((mix0, mix1))
    back_total = sum(b.astype(f32) for b in backs)
    sent_grads = own_half_first(back_total[:rows])
    gate_grads = (back_total[rows:, :rows] + back_total[rows:, rows : 2 * rows]).T

    inputs_all, ups_all, gate_up_all, act_all = held
    grad_halves = []
    for j in range(2):
        grad = jnp.concatenate(
            [dot_tn(inputs_all[j], gate_up_all[j]), dot_tn(ups_all[j], act_all[j])], 1
        ).astype(low)
        grad_halves.append(
            grad[: width // 2].astype(f32) + swap_on(grad[width // 2 :], "ctx", 2).astype(f32)
        )

    weighted = jnp.sum(gate_grads * gates, axis=1, keepdims=True)
    prob_grads = jnp.where(hits, (gate_grads - weighted) / sel_total, 0.0)
    logit_grads = probs * (prob_grads - jnp.sum(probs * prob_grads, axis=1, keepdims=True))
    router_float = router_weight.astype(f32)
    ffn_grads = sent_grads + jnp.dot(logit_grads, router_float.T, precision=lax.Precision.HIGHEST)
    router_grads = jnp.dot(ffn_low.astype(f32).T, logit_grads, precision=lax.Precision.HIGHEST)
    middle_grad = out_grad[0].astype(f32) + norm_backward(ffn_grads, middle_unit, middle_scale, gain_ffn)

    branch_grad = gather_ctx(by_exp(middle_grad.astype(low))).reshape(length, width)
    heads_grad = dot(branch_grad, weight_out).astype(low)
    joined_grads, gain_grads = attend_back(
        qkv, cosine, sine, doc_start, gains, attended, heads_grad, log_mass, heads
    )
    part_out = dot_tn(branch_grad, attended).astype(low)
    part_in = dot_tn(normed_seq, joined_grads).astype(low)
    normed_parts = dot_nt(joined_grads, weight_in).astype(low).reshape(n_ctx, rows, width)
    normed_grads = by_ctx(scatter_ctx(normed_parts))
    input_part = norm_backward(normed_grads, hidden_unit, hidden_scale, gain_attn)
    input_grad = (middle_grad + input_part).astype(low)[None]

    mixture = 0.0
    for s, (own, other) in enumerate(mixes):
        mix = add_low(own, swap_on(after(other, back_total), "ctx", 1))
        mixture = mixture + (mix if s == 0 else shift_back(mix, "exp", s)).astype(f32)
    mixture = own_half_first(mixture)
    output = (middle + mixture).astype(low)[None]

    kept = add_low(grad_halves[1], swap_on(grad_halves[0].astype(low), "grp", 1)).reshape(2, quarter, -1)
    mine, sibling = kept[0], swap_on(kept[1], "ctx", 1)
    mine_x, sibling_x = swap_on(mine, "grp", 1), swap_on(sibling, "grp", 1)
    totals = []
    for at in range(local_experts):
        same_core = at // 2 == core
        same_grp = at % 2 == grp
        totals.append(
            jnp.where(
                same_core, jnp.where(same_grp, mine, mine_x), jnp.where(same_grp, sibling, sibling_x)
            ).astype(f32)
        )
    total = jnp.stack(totals, 1)
    expert_in_grad = total[:, :, : 2 * hidden_units].reshape(expert_in.shape)
    expert_out_grad = total[:, :, 2 * hidden_units :]

    def to_rows(part):
        blocks = part.reshape(n_exp, n_ctx * shard, part.shape[1])
        own = pick(blocks, exp).astype(f32)
        for s in range(1, n_exp):
            own = own + shift_back(pick(blocks, (exp - s) % n_exp), "exp", s).astype(f32)
        own = own.astype(low).reshape(n_ctx, shard, part.shape[1])
        pieces = [pick(own, ctx)] + [swap_on(pick(own, ctx ^ m), "ctx", m) for m in range(1, n_ctx)]
        placed = place_ctx(pieces)
        return placed.astype(f32) + swap_on(placed, "grp", 1).astype(f32)

    rows_out = to_rows(part_out)
    rows_in = to_rows(part_in)
    attn_out_grad = rows_out.transpose(1, 0, 2).reshape(shard, query_width)
    wide = heads * head_dim
    attn_in_grad = jnp.concatenate(
        [
            rows_in[:, :, :wide].transpose(1, 0, 2).reshape(shard, query_width),
            rows_in[:, :, wide : wide + head_dim].transpose(1, 0, 2).reshape(shard, kv_width),
            rows_in[:, :, wide + head_dim :].transpose(1, 0, 2).reshape(shard, kv_width),
        ],
        1,
    )

    norm_gain_grads = jnp.stack(
        [jnp.sum(normed_grads * hidden_unit, axis=0), jnp.sum(ffn_grads * middle_unit, axis=0)], axis=1
    )
    small = [norm_gain_grads, gain_grads[:2].T, router_grads]
    summed = sum_all(jnp.concatenate([a.reshape(-1, head_dim) for a in small]))
    norm_total, head_total, router_total = (
        part.reshape(a.shape)
        for a, part in zip(
            small, jnp.split(summed, [norm_gain_grads.size // head_dim, norm_gain_grads.size // head_dim + 2])
        )
    )
    return (
        output,
        input_grad,
        attn_in_grad,
        attn_out_grad,
        norm_total,
        head_total,
        router_total,
        expert_in_grad,
        expert_out_grad,
    )


def solution(mesh):
    placed = (
        P(("grp", "exp"), "ctx", None),
        P(("grp", "exp"), "ctx", None),
        P(("grp", "exp"), None),
        P(("grp", "exp"), "ctx", None),
        P(("ctx", "exp"), None),
        P(("ctx", "exp"), None),
        P(),
        P(),
        P(),
        P("ctx", "exp", None, None),
        P("ctx", "exp", None),
    )
    sizes = dict(mesh.shape)
    body = per_device if sizes == {"grp": 2, "ctx": 4, "exp": 4} else per_device_general
    return jax.shard_map(
        body,
        mesh=mesh,
        in_specs=placed,
        out_specs=(
            P(("grp", "exp"), "ctx", None),
            P(("grp", "exp"), "ctx", None),
            P(("ctx", "exp"), None),
            P(("ctx", "exp"), None),
            P(),
            P(),
            P(),
            P("ctx", "exp", None, None),
            P("ctx", "exp", None),
        ),
        check_vma=False,
    )
```

```python
import functools

import jax
import jax.numpy as jnp
from jax import lax
from jax.experimental import pallas as pl
from jax.experimental.pallas import tpu as pltpu
from jax.sharding import PartitionSpec as P

epsilon = 1e-06
rotary_base = 1000000.0
key_span = 512


def doc_tables(lengths, positions):
    doc_ends = jnp.cumsum(lengths)
    passed = positions[:, None] >= doc_ends[None, :]
    doc_index = jnp.sum(passed.astype(jnp.int32), axis=1)
    first_pos = jnp.sum(jnp.where(passed, lengths[None, :], 0), axis=1)
    return (doc_index, positions - first_pos)


def rotate(values, relative, sign):
    half_dim = values.shape[-1] // 2
    freqs = rotary_base ** (-2.0 * jnp.arange(half_dim, dtype=jnp.float32) / values.shape[-1])
    angles = relative.astype(jnp.float32)[:, None] * freqs[None, :]
    cosine = jnp.cos(angles)[:, None, :]
    sine = sign * jnp.sin(angles)[:, None, :]
    first = values[..., :half_dim]
    second = values[..., half_dim:]
    return jnp.concatenate(
        [first * cosine - second * sine, second * cosine + first * sine], axis=-1
    )


def norm_forward(values, gain_vec):
    scale_vec = lax.rsqrt(jnp.mean(values * values, axis=-1, keepdims=True) + epsilon)
    unit_vec = values * scale_vec
    return (unit_vec * gain_vec, unit_vec, scale_vec)


def norm_backward(upstream, unit_vec, scale_vec, gain_vec):
    along = upstream * gain_vec
    return scale_vec * (along - unit_vec * jnp.mean(along * unit_vec, axis=-1, keepdims=True))


def per_device_general(
    hidden_in,
    out_grad,
    doc_lengths,
    routes,
    attention_input_weight,
    attn_out_weight,
    norm_gains,
    head_gains,
    router_weight,
    expert_in,
    expert_out,
):
    hidden = hidden_in[0].astype(jnp.float32)
    tokens_here, model_width = hidden.shape
    head_dim = head_gains.shape[0]
    expert_count = router_weight.shape[1]
    local_experts = expert_in.shape[1]
    route_picks = routes.shape[2]
    cycle_size = lax.axis_size("ctx")
    cycle_place = lax.axis_index("ctx")
    seq_length = tokens_here * cycle_size
    lengths = doc_lengths[0]
    query_pos = cycle_place * tokens_here + jnp.arange(tokens_here, dtype=jnp.int32)
    query_doc, query_rel = doc_tables(lengths, query_pos)
    gain_attn = norm_gains[:, 0].astype(jnp.float32)
    gain_ffn = norm_gains[:, 1].astype(jnp.float32)
    gain_query = head_gains[:, 0].astype(jnp.float32)
    gain_key = head_gains[:, 1].astype(jnp.float32)
    normed, hidden_unit, hidden_scale = norm_forward(hidden, gain_attn)
    normed_low = normed.astype(jnp.bfloat16)
    weight_in, weight_out = (
        lax.all_gather(attention_input_weight, ("ctx", "exp"), axis=0, tiled=True),
        lax.all_gather(attn_out_weight, ("ctx", "exp"), axis=0, tiled=True),
    )
    joined_projection = jnp.dot(normed_low, weight_in, preferred_element_type=jnp.float32)
    joined_width = weight_in.shape[1]
    query_width = weight_out.shape[1]
    head_count = query_width // head_dim
    kv_width = (joined_width - query_width) // 2
    kv_heads = kv_width // head_dim
    query_group_size = head_count // kv_heads
    query_raw = joined_projection[:, :query_width].reshape(tokens_here, head_count, head_dim)
    key_raw = joined_projection[:, query_width : query_width + kv_width].reshape(
        tokens_here, kv_heads, head_dim
    )
    value_low = joined_projection[:, query_width + kv_width :].astype(jnp.bfloat16)
    query_normed, query_unit, query_scale = norm_forward(query_raw, gain_query)
    key_normed, key_unit, key_scale = norm_forward(key_raw, gain_key)
    query_low = rotate(query_normed, query_rel, 1.0).astype(jnp.bfloat16)
    key_low = rotate(key_normed, query_rel, 1.0).astype(jnp.bfloat16)
    keys_local = jnp.stack([key_low.reshape(tokens_here, kv_width), value_low], axis=1)
    keys_all, in_all, out_all = (
        lax.all_gather(keys_local, "ctx", axis=0, tiled=True),
        lax.all_gather(expert_in, "ctx", axis=0, tiled=True),
        lax.all_gather(expert_out, "ctx", axis=0, tiled=True),
    )
    span = min(key_span, seq_length)
    block_count = seq_length // span
    key_blocks = keys_all.reshape(block_count, span, 2, kv_heads, head_dim)
    block_ids = jnp.arange(block_count, dtype=jnp.int32)
    query_rows = (
        query_low.reshape(tokens_here, kv_heads, query_group_size, head_dim)
        .transpose(1, 2, 0, 3)
        .reshape(kv_heads, query_group_size * tokens_here, head_dim)
    )
    score_scale = head_dim ** (-0.5)

    def block_scores(block_id, key_block):
        raw_scores = (
            jnp.einsum(
                "hrd,khd->hrk", query_rows, key_block[:, 0], preferred_element_type=jnp.float32
            )
            * score_scale
        )
        key_pos = block_id * span + jnp.arange(span, dtype=jnp.int32)
        key_doc = doc_tables(lengths, key_pos)[0]
        allowed = (key_pos[None, :] <= query_pos[:, None]) & (
            key_doc[None, :] == query_doc[:, None]
        )
        allowed = jnp.tile(allowed, (query_group_size, 1))[None]
        return (jnp.where(allowed, raw_scores, -1e30), allowed)

    def stats_step(running, scan_item):
        best_score, mass_sum = running
        block_id, key_block = scan_item
        masked, allowed = block_scores(block_id, key_block)
        new_best = jnp.maximum(best_score, jnp.max(masked, axis=-1))
        fresh = jnp.sum(jnp.where(allowed, jnp.exp(masked - new_best[..., None]), 0.0), axis=-1)
        return ((new_best, mass_sum * jnp.exp(best_score - new_best) + fresh), None)

    start_best = jnp.full((kv_heads, query_group_size * tokens_here), -1e30, jnp.float32)
    (best_score, mass_sum), unused = lax.scan(
        stats_step, (start_best, jnp.zeros_like(start_best)), (block_ids, key_blocks)
    )
    log_total = best_score + jnp.log(mass_sum)

    def value_step(summed, scan_item):
        block_id, key_block = scan_item
        masked, allowed = block_scores(block_id, key_block)
        weights = jnp.where(allowed, jnp.exp(masked - log_total[..., None]), 0.0).astype(
            jnp.bfloat16
        )
        return (
            summed
            + jnp.einsum(
                "hrk,khd->hrd", weights, key_block[:, 1], preferred_element_type=jnp.float32
            ),
            None,
        )

    start_rows = jnp.zeros((kv_heads, query_group_size * tokens_here, head_dim), jnp.float32)
    attended, unused = lax.scan(value_step, start_rows, (block_ids, key_blocks))
    attended_low = (
        attended.reshape(kv_heads, query_group_size, tokens_here, head_dim)
        .transpose(2, 0, 1, 3)
        .reshape(tokens_here, query_width)
        .astype(jnp.bfloat16)
    )
    branch = jnp.einsum("rc,dc->rd", attended_low, weight_out, preferred_element_type=jnp.float32)
    middle = hidden + branch
    ffn_normed, middle_unit, middle_scale = norm_forward(middle, gain_ffn)
    ffn_low = ffn_normed.astype(jnp.bfloat16)
    logits = jnp.dot(ffn_low, router_weight, preferred_element_type=jnp.float32)
    probs = jax.nn.softmax(logits, axis=-1)
    route_here = routes[0]
    route_hits = (
        route_here[:, :, None] == jnp.arange(expert_count, dtype=jnp.int32)[None, None, :]
    ).astype(jnp.float32)
    selected = jnp.sum(route_hits * probs[:, None, :], axis=-1)
    sel_total = jnp.sum(selected, axis=1, keepdims=True)
    gates = selected / sel_total
    capacity = 5 * tokens_here * route_picks // (4 * expert_count)
    flat_route = route_here.reshape(-1)
    slot_hits = (flat_route[:, None] == jnp.arange(expert_count, dtype=jnp.int32)[None, :]).astype(
        jnp.int32
    )
    slot_index = jnp.sum((jnp.cumsum(slot_hits, axis=0) - slot_hits) * slot_hits, axis=1)
    target = flat_route * capacity + slot_index
    exp_size = lax.axis_size("exp")
    buffer_shape = (exp_size, local_experts * capacity, model_width)
    arrive_shape = (exp_size, local_experts, capacity, model_width)
    empty_buffer = jnp.zeros((expert_count * capacity, model_width), jnp.bfloat16)
    outgoing = empty_buffer.at[target].set(jnp.repeat(ffn_low, route_picks, axis=0))
    arrived = lax.all_to_all(
        outgoing.reshape(buffer_shape), "exp", split_axis=0, concat_axis=0, tiled=True
    ).reshape(arrive_shape)
    gate_up = jnp.einsum("secd,dekf->seckf", arrived, in_all, preferred_element_type=jnp.float32)
    gate_part = gate_up[:, :, :, 0]
    up_part = gate_up[:, :, :, 1]
    sigmoid_part = jax.nn.sigmoid(gate_part)
    silu_part = jax.nn.silu(gate_part)
    act_low = (silu_part * up_part).astype(jnp.bfloat16)
    made = jnp.einsum(
        "secf,def->secd", act_low, out_all, preferred_element_type=jnp.float32
    ).astype(jnp.bfloat16)
    returned = lax.all_to_all(
        made.reshape(buffer_shape), "exp", split_axis=0, concat_axis=0, tiled=True
    ).reshape(expert_count * capacity, model_width)
    route_out = returned[target].astype(jnp.float32).reshape(tokens_here, route_picks, model_width)
    mixture = jnp.sum(gates[:, :, None] * route_out, axis=1)
    output = (middle + mixture).astype(jnp.bfloat16)[None]
    upstream = out_grad[0].astype(jnp.float32)
    gate_grads = jnp.sum(upstream[:, None, :] * route_out, axis=-1)
    route_grads = (
        (gates[:, :, None] * upstream[:, None, :])
        .astype(jnp.bfloat16)
        .reshape(tokens_here * route_picks, model_width)
    )
    outgoing_grads = empty_buffer.at[target].set(route_grads)
    grads_arrived = lax.all_to_all(
        outgoing_grads.reshape(buffer_shape), "exp", split_axis=0, concat_axis=0, tiled=True
    ).reshape(arrive_shape)
    act_grads = jnp.einsum(
        "secd,def->secf", grads_arrived, out_all, preferred_element_type=jnp.float32
    )
    gate_grad_part = act_grads * up_part * sigmoid_part * (1.0 + gate_part * (1.0 - sigmoid_part))
    gate_up_grads = jnp.stack([gate_grad_part, act_grads * silu_part], axis=3).astype(jnp.bfloat16)
    input_rows = jnp.einsum(
        "seckf,dekf->secd", gate_up_grads, in_all, preferred_element_type=jnp.float32
    ).astype(jnp.bfloat16)
    came_back = lax.all_to_all(
        input_rows.reshape(buffer_shape), "exp", split_axis=0, concat_axis=0, tiled=True
    ).reshape(expert_count * capacity, model_width)
    sent_grads = jnp.sum(
        came_back[target].astype(jnp.float32).reshape(tokens_here, route_picks, model_width), axis=1
    )
    term_in = jnp.einsum(
        "secd,seckf->dekf", arrived, gate_up_grads, preferred_element_type=jnp.float32
    )
    term_out = jnp.einsum(
        "secd,secf->def", grads_arrived, act_low, preferred_element_type=jnp.float32
    )
    expert_local = lax.psum_scatter(
        jnp.concatenate([term_in, term_out[:, :, None, :]], axis=2).astype(jnp.bfloat16),
        "ctx",
        scatter_dimension=0,
        tiled=True,
    )
    weighted = jnp.sum(gate_grads * gates, axis=1, keepdims=True)
    sel_grads = (gate_grads - weighted) / sel_total
    prob_grads = jnp.sum(sel_grads[:, :, None] * route_hits, axis=1)
    logit_grads = probs * (prob_grads - jnp.sum(probs * prob_grads, axis=1, keepdims=True))
    router_float = router_weight.astype(jnp.float32)
    ffn_grads = sent_grads + jnp.dot(logit_grads, router_float.T, precision=lax.Precision.HIGHEST)
    router_grads = jnp.dot(
        ffn_low.astype(jnp.float32).T, logit_grads, precision=lax.Precision.HIGHEST
    )
    middle_grad = upstream + norm_backward(ffn_grads, middle_unit, middle_scale, gain_ffn)
    attn_grad_low = middle_grad.astype(jnp.bfloat16)
    heads_grad_low = jnp.dot(attn_grad_low, weight_out, preferred_element_type=jnp.float32).astype(
        jnp.bfloat16
    )
    grad_rows = (
        heads_grad_low.reshape(tokens_here, kv_heads, query_group_size, head_dim)
        .transpose(1, 2, 0, 3)
        .reshape(kv_heads, query_group_size * tokens_here, head_dim)
    )

    def delta_step(summed, scan_item):
        block_id, key_block = scan_item
        masked, allowed = block_scores(block_id, key_block)
        weights = jnp.where(allowed, jnp.exp(masked - log_total[..., None]), 0.0)
        weight_grads = jnp.einsum(
            "hrd,khd->hrk", grad_rows, key_block[:, 1], preferred_element_type=jnp.float32
        )
        return (summed + jnp.sum(weights * weight_grads, axis=-1), None)

    delta_sum, unused = lax.scan(delta_step, jnp.zeros_like(log_total), (block_ids, key_blocks))

    def grad_step(query_grads, scan_item):
        block_id, key_block = scan_item
        masked, allowed = block_scores(block_id, key_block)
        weights = jnp.where(allowed, jnp.exp(masked - log_total[..., None]), 0.0)
        weight_grads = jnp.einsum(
            "hrd,khd->hrk", grad_rows, key_block[:, 1], preferred_element_type=jnp.float32
        )
        score_grads = (weights * (weight_grads - delta_sum[..., None])).astype(jnp.bfloat16)
        query_grads = (
            query_grads
            + jnp.einsum(
                "hrk,khd->hrd", score_grads, key_block[:, 0], preferred_element_type=jnp.float32
            )
            * score_scale
        )
        key_grads = (
            jnp.einsum("hrk,hrd->khd", score_grads, query_rows, preferred_element_type=jnp.float32)
            * score_scale
        )
        value_grads = jnp.einsum(
            "hrk,hrd->khd",
            weights.astype(jnp.bfloat16),
            grad_rows,
            preferred_element_type=jnp.float32,
        )
        return (query_grads, jnp.stack([key_grads, value_grads], axis=1))

    query_grads, block_grads = lax.scan(grad_step, start_rows, (block_ids, key_blocks))
    key_value_grads = lax.psum_scatter(
        block_grads.reshape(seq_length, 2, kv_width).astype(jnp.bfloat16),
        "ctx",
        scatter_dimension=0,
        tiled=True,
    ).astype(jnp.float32)
    query_grads = (
        query_grads.reshape(kv_heads, query_group_size, tokens_here, head_dim)
        .transpose(2, 0, 1, 3)
        .reshape(tokens_here, head_count, head_dim)
    )
    query_turned = rotate(query_grads, query_rel, -1.0)
    query_proj = norm_backward(query_turned, query_unit, query_scale, gain_query)
    key_turned = rotate(
        key_value_grads[:, 0].reshape(tokens_here, kv_heads, head_dim), query_rel, -1.0
    )
    key_proj = norm_backward(key_turned, key_unit, key_scale, gain_key)
    head_gain_grads = jnp.stack(
        [
            jnp.sum(query_turned * query_unit, axis=(0, 1)),
            jnp.sum(key_turned * key_unit, axis=(0, 1)),
        ],
        axis=1,
    )
    joined_grads = jnp.concatenate(
        [
            query_proj.reshape(tokens_here, query_width),
            key_proj.reshape(tokens_here, kv_width),
            key_value_grads[:, 1],
        ],
        axis=1,
    ).astype(jnp.bfloat16)
    normed_grads = jnp.einsum(
        "rc,dc->rd", joined_grads, weight_in, preferred_element_type=jnp.float32
    )
    input_part = norm_backward(normed_grads, hidden_unit, hidden_scale, gain_attn)
    input_grad = (middle_grad + input_part).astype(jnp.bfloat16)[None]
    norm_gain_grads = jnp.stack(
        [jnp.sum(normed_grads * hidden_unit, axis=0), jnp.sum(ffn_grads * middle_unit, axis=0)],
        axis=1,
    )
    norm_total, head_total, router_total = lax.psum(
        (norm_gain_grads, head_gain_grads, router_grads), ("grp", "ctx", "exp")
    )
    part_in = jnp.einsum("rc,rq->cq", normed_low, joined_grads, preferred_element_type=jnp.float32)
    part_out = jnp.einsum(
        "rc,rq->cq", attn_grad_low, attended_low, preferred_element_type=jnp.float32
    )
    dense_local = lax.psum_scatter(
        jnp.concatenate([part_in, part_out], axis=1),
        ("ctx", "exp"),
        scatter_dimension=0,
        tiled=True,
    )
    dense_total, expert_total = (
        lax.psum(dense_local.astype(jnp.bfloat16), "grp").astype(jnp.float32),
        lax.psum(expert_local, "grp").astype(jnp.float32),
    )
    return (
        output,
        input_grad,
        dense_total[:, :joined_width],
        dense_total[:, joined_width:],
        norm_total,
        head_total,
        router_total,
        expert_total[:, :, :2],
        expert_total[:, :, 2],
    )


NT = (((1,), (1,)), ((), ()))

def head_norm(raw):
    scale = lax.rsqrt(jnp.mean(raw * raw, axis=-1, keepdims=True) + epsilon)
    return raw * scale, scale

def turn(values, cosine, sine):
    return values * cosine + pltpu.roll(values, values.shape[-1] // 2, 1) * sine

def dots(a, b):
    return jnp.dot(a, b, preferred_element_type=jnp.float32)

def dots_nt(a, b):
    return lax.dot_general(a, b, NT, preferred_element_type=jnp.float32)

def allowed_chunk(start, i, j, tile):
    key_pos = j * tile + lax.broadcasted_iota(jnp.int32, (tile, tile), 0)
    ok = key_pos >= start
    if i == j:
        query_pos = i * tile + lax.broadcasted_iota(jnp.int32, (tile, tile), 1)
        ok = ok & (key_pos <= query_pos)
    return ok

def attend_kernel(tile, q_ref, k_ref, v_ref, cos_ref, sin_ref, start_ref, gain_ref,
                  o_ref, lse_ref, key_s, value_t):
    length, head_dim = q_ref.shape
    c = head_dim ** -0.5 * 1.4426950408889634
    @pl.when(pl.program_id(0) == 0)
    def _():
        unit, _ = head_norm(k_ref[...])
        key_s[...] = turn(unit * gain_ref[1:2], cos_ref[...], sin_ref[...]).astype(jnp.bfloat16)
        value_t[...] = v_ref[...].T.astype(jnp.bfloat16)
    unit, _ = head_norm(q_ref[...])
    query = turn(unit * gain_ref[0:1], cos_ref[...], sin_ref[...]).astype(jnp.bfloat16)
    for i in range(length // tile):
        rows = slice(i * tile, (i + 1) * tile)
        start = start_ref[:, rows]
        mass = jnp.zeros((1, tile), jnp.float32)
        total = jnp.zeros((head_dim, tile), jnp.float32)
        for j in range(i + 1):
            cols = slice(j * tile, (j + 1) * tile)
            s = dots_nt(key_s[cols, :], query[rows])
            p = jnp.where(allowed_chunk(start, i, j, tile), jnp.exp2(s * c), 0.0)
            mass = mass + jnp.sum(p, axis=0, keepdims=True)
            total = total + dots(value_t[:, cols], p.astype(jnp.bfloat16))
        o_ref[rows, :] = (total / mass).T.astype(jnp.bfloat16)
        lse_ref[0, :, rows] = jnp.log2(mass)

def attend(qkv, cosine, sine, start, gains, heads):
    length, head_dim = cosine.shape
    full = lambda shape: pl.BlockSpec(shape, lambda h: (0, 0))
    col = lambda at: pl.BlockSpec((length, head_dim), lambda h: (0, at))
    return pl.pallas_call(
        functools.partial(attend_kernel, min(256, length)),
        grid=(heads,),
        in_specs=[
            pl.BlockSpec((length, head_dim), lambda h: (0, h)), col(heads), col(heads + 1),
            full((length, head_dim)), full((length, head_dim)), full((1, length)), full(gains.shape),
        ],
        out_specs=[
            pl.BlockSpec((length, head_dim), lambda h: (0, h)),
            pl.BlockSpec((1, 1, length), lambda h: (h, 0, 0)),
        ],
        out_shape=[
            jax.ShapeDtypeStruct((length, heads * head_dim), jnp.bfloat16),
            jax.ShapeDtypeStruct((heads, 1, length), jnp.float32),
        ],
        scratch_shapes=[
            pltpu.VMEM((length, head_dim), jnp.bfloat16),
            pltpu.VMEM((head_dim, length), jnp.bfloat16),
        ],
        compiler_params=pltpu.CompilerParams(vmem_limit_bytes=48 * 2**20),
    )(qkv, qkv, qkv, cosine, sine, start, gains)

def attend_back_kernel(tile, heads, q_ref, k_ref, v_ref, cos_ref, sin_ref, start_ref, gain_ref,
                       o_ref, go_ref, lse_ref, grad_ref, gain_grad_ref,
                       key_s, key_t, value_s, key_grad, value_grad, query_grad):
    length, head_dim = q_ref.shape
    scale = head_dim ** -0.5
    c = scale * 1.4426950408889634
    step = pl.program_id(0)

    def norm_back(turned_grad, raw, row):
        back = turn(turned_grad, cos_ref[...], -sin_ref[...])
        unit, unit_scale = head_norm(raw)
        gain_grad_ref[row:row + 1] += jnp.sum(back * unit, axis=0, keepdims=True)
        along = back * gain_ref[row:row + 1]
        return unit_scale * (along - unit * jnp.mean(along * unit, axis=-1, keepdims=True))

    @pl.when(step == 0)
    def _():
        unit, _ = head_norm(k_ref[...])
        key = turn(unit * gain_ref[1:2], cos_ref[...], sin_ref[...])
        key_s[...] = key.astype(jnp.bfloat16)
        key_t[...] = key.T.astype(jnp.bfloat16)
        value_s[...] = v_ref[...].astype(jnp.bfloat16)
        key_grad[...] = jnp.zeros_like(key_grad)
        value_grad[...] = jnp.zeros_like(value_grad)
        gain_grad_ref[...] = jnp.zeros_like(gain_grad_ref)

    @pl.when(step < heads)
    def _():
        unit, _ = head_norm(q_ref[...])
        query = turn(unit * gain_ref[0:1], cos_ref[...], sin_ref[...]).astype(jnp.bfloat16)
        for i in range(length // tile):
            rows = slice(i * tile, (i + 1) * tile)
            start = start_ref[:, rows]
            lse = lse_ref[0, :, rows]
            up = go_ref[rows, :]
            delta = jnp.sum((up.astype(jnp.float32) * o_ref[rows, :].astype(jnp.float32)).T, axis=0, keepdims=True)
            q_i = query[rows]
            total = jnp.zeros((head_dim, tile), jnp.float32)
            for j in range(i + 1):
                cols = slice(j * tile, (j + 1) * tile)
                s = dots_nt(key_s[cols, :], q_i)
                p = jnp.where(allowed_chunk(start, i, j, tile), jnp.exp2(s * c - lse), 0.0)
                dp = dots_nt(value_s[cols, :], up)
                ds = (p * (dp - delta)).astype(jnp.bfloat16)
                value_grad[cols, :] += dots(p.astype(jnp.bfloat16), up)
                key_grad[cols, :] += dots(ds, q_i)
                total = total + dots(key_t[:, cols], ds)
            query_grad[rows, :] = (total * scale).T
        grad_ref[...] = norm_back(query_grad[...], q_ref[...], 0).astype(jnp.bfloat16)

    @pl.when(step == heads)
    def _():
        grad_ref[...] = norm_back(key_grad[...] * scale, k_ref[...], 1).astype(jnp.bfloat16)

    @pl.when(step == heads + 1)
    def _():
        grad_ref[...] = value_grad[...].astype(jnp.bfloat16)

def attend_back(qkv, cosine, sine, start, gains, attended, upstream, lse, heads):
    length, head_dim = cosine.shape
    full = lambda shape: pl.BlockSpec(shape, lambda h: (0, 0))
    col = lambda at: pl.BlockSpec((length, head_dim), lambda h: (0, at))
    per_head = pl.BlockSpec((length, head_dim), lambda h: (0, jnp.minimum(h, heads - 1)))
    return pl.pallas_call(
        functools.partial(attend_back_kernel, min(256, length), heads),
        grid=(heads + 2,),
        in_specs=[
            per_head, col(heads), col(heads + 1),
            full((length, head_dim)), full((length, head_dim)), full((1, length)), full(gains.shape),
            per_head, per_head,
            pl.BlockSpec((1, 1, length), lambda h: (jnp.minimum(h, heads - 1), 0, 0)),
        ],
        out_specs=[
            pl.BlockSpec((length, head_dim), lambda h: (0, h)),
            full((8, head_dim)),
        ],
        out_shape=[
            jax.ShapeDtypeStruct((length, (heads + 2) * head_dim), jnp.bfloat16),
            jax.ShapeDtypeStruct((8, head_dim), jnp.float32),
        ],
        scratch_shapes=[
            pltpu.VMEM((length, head_dim), jnp.bfloat16),
            pltpu.VMEM((head_dim, length), jnp.bfloat16),
            pltpu.VMEM((length, head_dim), jnp.bfloat16),
            pltpu.VMEM((length, head_dim), jnp.float32),
            pltpu.VMEM((length, head_dim), jnp.float32),
            pltpu.VMEM((length, head_dim), jnp.float32),
        ],
        compiler_params=pltpu.CompilerParams(vmem_limit_bytes=48 * 2**20),
    )(qkv, qkv, qkv, cosine, sine, start, gains, attended, upstream, lse)


def front_kernel(
    n_ctx, n_exp, heads,
    win, wout, normed, expert_rows, ups, hidden, gain2, cos_ref, sin_ref, start_ref, gain_ref,
    wi_out, wo_out, xn_out, qkv_out, att_out, pieces, upb, tokb, lse_ref, middle_ref,
    wi, wo, xn, qkv, att, part, got_core, got_over, hn, key_s, value_t, send, recv, local,
):
    grp, ctx, exp = lax.axis_index("grp"), lax.axis_index("ctx"), lax.axis_index("exp")
    core = ctx % 2
    shard = win.shape[0] // n_ctx
    rows = normed.shape[0]
    head_dim = cos_ref.shape[1]
    block = n_ctx * shard
    half = block // 2
    names = {}

    def place(name):
        return names.setdefault(name, len(names))

    waits = []

    def move(name, src, dst, to, landed, ok=True, landed_ok=True):
        i = place(name)
        out = pltpu.make_async_remote_copy(src, dst, send.at[i], recv.at[i], device_id=to)
        come = pltpu.make_async_remote_copy(src, landed, send.at[i], recv.at[i], device_id=to)
        def start():
            when(ok, out.start)
        def arrive():
            when(landed_ok, come.wait_recv)
        waits.append(lambda: when(ok, out.wait_send))
        return start, arrive

    def when(ok, f):
        if ok is True:
            f()
        else:
            pl.when(ok)(lambda: f())

    def keep(i, src, dst):
        return pltpu.make_async_copy(src, dst, local.at[i])

    mates = {1: {"ctx": ctx ^ 1}, 2: {"ctx": ctx ^ 2}, 3: {"ctx": ctx ^ 3}}
    other_grp, right, left = {"grp": 1 - grp}, {"exp": exp + 1}, {"exp": exp - 1}
    has_right, has_left = exp < n_exp - 1, exp > 0

    barrier = pltpu.get_barrier_semaphore()
    for to in (mates[1], mates[2], mates[3], other_grp):
        pl.semaphore_signal(barrier, inc=1, device_id=to)
    pl.when(has_right)(lambda: pl.semaphore_signal(barrier, inc=1, device_id=right))
    pl.when(has_left)(lambda: pl.semaphore_signal(barrier, inc=1, device_id=left))
    pl.semaphore_wait(barrier, 4 + has_right.astype(jnp.int32) + has_left.astype(jnp.int32))

    def rows_of(ref, index, size):
        return ref.at[pl.ds(pl.multiple_of(index * size, size), size)]

    owns = [
        keep(0, rows_of(win, ctx, shard), rows_of(wi, exp * n_ctx + ctx, shard)),
        keep(1, rows_of(wout, ctx, shard), rows_of(wo, exp * n_ctx + ctx, shard)),
        keep(2, normed, rows_of(xn, ctx, rows)),
        keep(3, ups, upb.at[0, 0]),
    ]
    here = [2 * core + 1 - grp, 2 * core + grp]
    there = [2 * (1 - core) + 1 - grp, 2 * (1 - core) + grp]
    owns += [keep(4 + j, expert_rows.at[here[j]], pieces.at[j, 0]) for j in range(2)]

    def exchange(name, src, buf):
        return [
            move(name + str(m), rows_of(src, ctx ^ m, shard), rows_of(buf, exp * n_ctx + ctx, shard),
                 mates[m], rows_of(buf, exp * n_ctx + (ctx ^ m), shard))
            for m in (2, 3, 1)
        ]

    give_in, give_out = exchange("in", win, wi), exchange("out", wout, wo)

    def line(name, buf):
        at = lambda b, g: rows_of(buf, b * 2 + g, half)
        steps = []
        for s in range(1, n_exp):
            r = move(name + "r" + str(s), at(exp - s + 1, grp), at(exp - s + 1, grp), right, at(exp - s, grp),
                     has_right & (exp >= s - 1), exp >= s)
            l = move(name + "l" + str(s), at(exp + s - 1, grp), at(exp + s - 1, grp), left, at(exp + s, grp),
                     has_left & (exp + s - 1 < n_exp), exp + s < n_exp)
            rx = move(name + "rx" + str(s), at(exp - s, grp), at(exp - s, grp), other_grp, at(exp - s, 1 - grp),
                      exp >= s, exp >= s)
            lx = move(name + "lx" + str(s), at(exp + s, grp), at(exp + s, grp), other_grp, at(exp + s, 1 - grp),
                      exp + s < n_exp, exp + s < n_exp)
            steps.append((r, l, rx, lx))
        return steps

    line_in, line_out = line("in", wi), line("out", wo)

    def begin(steps, s):
        steps[s - 1][0][0]()
        steps[s - 1][1][0]()

    def relay(steps, s):
        for way in (0, 1):
            steps[s - 1][way][1]()
            if s < n_exp - 1:
                steps[s][way][0]()
            steps[s - 1][2 + way][0]()

    def crossed(steps):
        for s in range(1, n_exp):
            steps[s - 1][2][1]()
            steps[s - 1][3][1]()

    def tokens(name, own, buf):
        steps = []
        for s in range(1, n_exp):
            r = move(name + "r" + str(s), own if s == 1 else buf.at[s - 1, 0], buf.at[s, 0], right, buf.at[s, 0],
                     has_right & (exp >= s - 1), exp >= s)
            l = move(name + "l" + str(s), own if s == 1 else buf.at[n_exp - s + 1, 0], buf.at[n_exp - s, 0], left,
                     buf.at[n_exp - s, 0], has_left & (exp + s - 1 < n_exp), exp + s < n_exp)
            steps.append((r, l))
        own_core = move(name + "c", own, buf.at[0, 1], mates[1], buf.at[0, 1])
        rc = {}
        for s in range(1, n_exp):
            rc[s] = (
                move(name + "rc" + str(s), buf.at[s, 0], buf.at[s, 1], mates[1], buf.at[s, 1], exp >= s, exp >= s),
                move(name + "lc" + str(s), buf.at[n_exp - s, 0], buf.at[n_exp - s, 1], mates[1],
                     buf.at[n_exp - s, 1], exp + s < n_exp, exp + s < n_exp),
            )
        return steps, own_core, rc

    def token_begin(t, s):
        t[0][s - 1][0][0]()
        t[0][s - 1][1][0]()

    def token_arrive(t, s):
        for way in (0, 1):
            t[0][s - 1][way][1]()
            t[2][s][way][0]()

    def token_end(t):
        t[1][1]()
        for s in range(1, n_exp):
            t[2][s][0][1]()
            t[2][s][1][1]()

    up_line = tokens("up", ups, upb)
    tok_line = tokens("tok", hn, tokb)

    xn_over = move("xo", normed, rows_of(xn, ctx, rows), mates[2], rows_of(xn, ctx ^ 2, rows))
    xn_core = move("xc", normed, rows_of(xn, ctx, rows), mates[1], rows_of(xn, ctx ^ 1, rows))
    xn_both = move("xb", rows_of(xn, ctx ^ 2, rows), rows_of(xn, ctx ^ 2, rows), mates[1], rows_of(xn, ctx ^ 3, rows))

    sib = [move("es" + str(j), expert_rows.at[there[j]], pieces.at[j, 1], mates[1], pieces.at[j, 1]) for j in range(2)]
    over_same = move("eo", expert_rows.at[here[0]], pieces.at[0, 2], mates[2], pieces.at[0, 2])
    over_other = move("ep", expert_rows.at[there[0]], pieces.at[0, 3], mates[3], pieces.at[0, 3])
    cross_same = move("ex", pieces.at[0, 2], pieces.at[1, 2], other_grp, pieces.at[1, 2])
    cross_other = move("ey", pieces.at[0, 3], pieces.at[1, 3], other_grp, pieces.at[1, 3])

    part_of = lambda m: rows_of(part, ctx ^ m, rows)
    core_sums = [move("p" + str(m), part_of(m), got_core.at[i], mates[1], got_core.at[i]) for i, m in enumerate((1, 3))]
    over_sum = move("po", part_of(2), got_over, mates[2], got_over)

    for c in owns:
        c.start()
    for start, _ in give_in:
        start()
    token_begin(up_line, 1)
    up_line[1][0]()
    owns[0].wait()
    for _, arrive in give_in:
        arrive()
    begin(line_in, 1)
    xn_over[0]()
    xn_core[0]()
    for start, _ in give_out:
        start()
    relay(line_in, 1)
    relay(line_in, 2)
    owns[1].wait()
    for _, arrive in give_out:
        arrive()
    xn_over[1]()
    xn_both[0]()
    over_same[0]()
    sib[0][0]()
    sib[1][0]()
    relay(line_in, 3)
    begin(line_out, 1)
    token_arrive(up_line, 1)
    crossed(line_in)
    owns[2].wait()
    xn_core[1]()
    xn_both[1]()

    c = head_dim ** -0.5 * 1.4426950408889634
    length = xn.shape[0]
    tile = min(256, length)
    wide = heads * head_dim
    kv = dots(xn[...], wi[:, wide:])
    qkv[:, wide:] = kv
    unit, _ = head_norm(kv[:, :head_dim])
    key_s[...] = turn(unit * gain_ref[1:2], cos_ref[...], sin_ref[...]).astype(jnp.bfloat16)
    value_t[...] = kv[:, head_dim:].T.astype(jnp.bfloat16)

    def pair(p, carry):
        cols = pl.ds(pl.multiple_of(p * 2 * head_dim, 2 * head_dim), 2 * head_dim)
        raw2 = dots(xn[...], wi[:, cols])
        qkv[:, cols] = raw2
        for hh in range(2):
            unit, _ = head_norm(raw2[:, hh * head_dim : (hh + 1) * head_dim])
            query = turn(unit * gain_ref[0:1], cos_ref[...], sin_ref[...]).astype(jnp.bfloat16)
            for i in range(length // tile):
                at = slice(i * tile, (i + 1) * tile)
                start = start_ref[:, at]
                mass = jnp.zeros((1, tile), jnp.float32)
                total = jnp.zeros((head_dim, tile), jnp.float32)
                for j in range(i + 1):
                    keys = slice(j * tile, (j + 1) * tile)
                    s = dots_nt(key_s[keys, :], query[at])
                    w = jnp.where(allowed_chunk(start, i, j, tile), jnp.exp2(s * c), 0.0)
                    mass = mass + jnp.sum(w, axis=0, keepdims=True)
                    total = total + dots(value_t[:, keys], w.astype(jnp.bfloat16))
                att[at, pl.ds(pl.multiple_of((2 * p + hh) * head_dim, head_dim), head_dim)] = (
                    (total / mass).T.astype(jnp.bfloat16)
                )
                lse_ref[2 * p + hh, :, at] = jnp.log2(mass)
        return carry

    relay(line_out, 1)
    lax.fori_loop(0, heads // 4, pair, 0)
    relay(line_out, 2)
    lax.fori_loop(heads // 4, heads // 2, pair, 0)
    relay(line_out, 3)
    token_begin(up_line, 2)
    over_same[1]()
    cross_same[0]()
    over_other[0]()
    crossed(line_out)
    keeps = [
        keep(6, wi, wi_out), keep(7, wo, wo_out), keep(8, xn, xn_out), keep(9, qkv, qkv_out), keep(10, att, att_out)
    ]
    for k in keeps:
        k.start()

    def project(m):
        at = pl.ds(pl.multiple_of((ctx ^ m) * rows, rows), rows)
        def columns(n, carry):
            cols = pl.ds(pl.multiple_of(n * 2 * tile, 2 * tile), 2 * tile)
            part[at, cols] = dots_nt(att[at, :], wo[cols, :]).astype(jnp.bfloat16)
            return carry
        lax.fori_loop(0, part.shape[1] // (2 * tile), columns, 0)

    project(1)
    core_sums[0][0]()
    project(3)
    core_sums[1][0]()
    project(2)
    core_sums[1][1]()
    two = pl.ds(pl.multiple_of((ctx ^ 2) * rows, rows), rows)
    part[two, :] = (part[two, :].astype(jnp.float32) + got_core[1].astype(jnp.float32)).astype(jnp.bfloat16)
    over_sum[0]()
    project(0)
    core_sums[0][1]()
    token_arrive(up_line, 2)
    token_begin(up_line, 3)
    own = pl.ds(pl.multiple_of(ctx * rows, rows), rows)
    middle_ref[...] = hidden[...].astype(jnp.float32) + part[own, :].astype(jnp.float32) + got_core[0].astype(jnp.float32)
    over_sum[1]()
    middle = middle_ref[...] + got_over[...].astype(jnp.float32)
    middle_ref[...] = middle
    scale = lax.rsqrt(jnp.mean(middle * middle, axis=-1, keepdims=True) + epsilon)
    normed2 = (middle * scale * gain2[...]).astype(jnp.bfloat16)
    for b in range(n_exp):
        for a in range(n_ctx):
            to = (a * n_exp + b) * shard
            at = pl.multiple_of((to + (ctx // 2) * (block * n_exp // 2)) % (block * n_exp), shard)
            hn[:, pl.ds(at, shard)] = normed2[:, (b * n_ctx + a) * shard : (b * n_ctx + a + 1) * shard]
    token_begin(tok_line, 1)
    tok_line[1][0]()
    mine = keep(11, hn, tokb.at[0, 0])
    mine.start()
    token_arrive(up_line, 3)
    token_arrive(tok_line, 1)
    token_begin(tok_line, 2)
    over_other[1]()
    cross_other[0]()
    token_arrive(tok_line, 2)
    token_begin(tok_line, 3)
    token_arrive(tok_line, 3)
    token_end(up_line)
    token_end(tok_line)
    sib[0][1]()
    sib[1][1]()
    cross_same[1]()
    cross_other[1]()
    for k in owns[3:] + keeps + [mine]:
        k.wait()
    for w in waits:
        w()


def front_count(n_exp):
    return 3 + 3 + 8 * (n_exp - 1) + 2 * (4 * (n_exp - 1) + 1) + 3 + 2 + 4 + 3


def front(win, wout, normed, expert_rows, ups, hidden, gain2, cosine, sine, start, gains, heads, n_ctx, n_exp):
    rows, width = normed.shape
    length, head_dim = cosine.shape
    low, f32 = jnp.bfloat16, jnp.float32
    struct = jax.ShapeDtypeStruct
    anywhere = pl.BlockSpec(memory_space=pl.ANY)
    vmem = pl.BlockSpec(memory_space=pltpu.VMEM)
    cols_in, cols_out = win.shape[1], wout.shape[1]
    quarter, wide3 = expert_rows.shape[1:]
    ext = ups.shape[0]
    count = front_count(n_exp)
    return pl.pallas_call(
        functools.partial(front_kernel, n_ctx, n_exp, heads),
        in_specs=[anywhere] * 5 + [vmem] * 6,
        out_specs=[anywhere] * 8 + [vmem] * 2,
        out_shape=[
            struct((width, cols_in), low), struct((width, cols_out), low), struct((length, width), low),
            struct((length, cols_in), f32), struct((length, cols_out), low),
            struct((2, n_ctx, quarter, wide3), low),
            struct((n_exp, 2, ext, width), low), struct((n_exp, 2, rows, width), low),
            struct((heads, 1, length), f32), struct((rows, width), f32),
        ],
        scratch_shapes=[
            pltpu.VMEM((width, cols_in), low), pltpu.VMEM((width, cols_out), low), pltpu.VMEM((length, width), low),
            pltpu.VMEM((length, cols_in), f32), pltpu.VMEM((length, cols_out), low), pltpu.VMEM((length, width), low),
            pltpu.VMEM((2, rows, width), low), pltpu.VMEM((rows, width), low), pltpu.VMEM((rows, width), low),
            pltpu.VMEM((length, head_dim), low), pltpu.VMEM((head_dim, length), low),
            pltpu.SemaphoreType.DMA((count,)), pltpu.SemaphoreType.DMA((count,)), pltpu.SemaphoreType.DMA((12,)),
        ],
        compiler_params=pltpu.CompilerParams(
            collective_id=0, has_side_effects=True, vmem_limit_bytes=60 * 2**20
        ),
    )(win, wout, normed, expert_rows, ups, hidden, gain2, cosine, sine, start, gains)


def expert_kernel(blocks, capacity, piece_count, *refs):
    tok0, tok1, up0, up1, router_ref = refs[:5]
    weights = refs[5 : 5 + 6 * piece_count]
    x_out, up_out, gug_out, act_out, sent0, sent1, mix0, mix1 = refs[-18:-10]
    x_s, up_s, table_s, gate_s, y_acc, sent_acc, gg_acc, gate_tab0, gate_tab1, gg_rows = refs[-10:]
    tokens, ups = (tok0, tok1), (up0, up1)
    rows = tok0.shape[0]
    span = tok0.shape[1] // piece_count
    half = capacity
    ctx, grp, exp = lax.axis_index("ctx"), lax.axis_index("grp"), lax.axis_index("exp")
    core = ctx % 2
    step_e, step_f = pl.program_id(0), pl.program_id(1)
    experts = router_ref.shape[0]
    expert = exp * 4 + 2 * core + jnp.where(step_e == 0, 1 - grp, grp)
    order = [pl.ds(pl.multiple_of((q ^ core) * span, span), span) for q in range(piece_count)]

    @pl.when((step_e == 0) & (step_f == 0))
    def _():
        gg_rows[...] = jnp.zeros_like(gg_rows)
        for kk, tab in enumerate((gate_tab0, gate_tab1)):
            logits = dots_nt(router_ref[...], tokens[kk][...])
            powers = jnp.exp(logits - jnp.max(logits, axis=0, keepdims=True))
            probs = powers / jnp.sum(powers, axis=0, keepdims=True)
            slot = ups[kk][rows:, :rows].astype(jnp.float32)
            chosen = jnp.where(slot >= 0, probs, 0.0)
            tab[...] = chosen / jnp.sum(chosen, axis=0, keepdims=True)

    @pl.when(step_f == 0)
    def _():
        y_acc[...] = jnp.zeros_like(y_acc)
        sent_acc[...] = jnp.zeros_like(sent_acc)
        gg_acc[...] = jnp.zeros_like(gg_acc)
        which = lax.broadcasted_iota(jnp.int32, (experts, rows), 0) == expert
        for kk, tab in enumerate((gate_tab0, gate_tab1)):
            slots = ups[kk][rows:, :rows].astype(jnp.float32)
            slot = jnp.sum(jnp.where(which, slots, 0.0), axis=0, keepdims=True)
            gate = jnp.sum(jnp.where(which, tab[...], 0.0), axis=0, keepdims=True)
            table = slot == lax.broadcasted_iota(jnp.int32, (capacity, rows), 0).astype(jnp.float32)
            table_low = jnp.where(table, 1.0, 0.0).astype(jnp.bfloat16)
            table_s[kk] = table_low
            at = slice(kk * half, (kk + 1) * half)
            gate_s[at, :] = jnp.sum(jnp.where(table, gate, 0.0), axis=1, keepdims=True)
            for q in range(piece_count):
                cols = slice(q * span, (q + 1) * span)
                x_s[at, cols] = dots(table_low, tokens[kk][:, order[q]]).astype(jnp.bfloat16)
                up_s[at, cols] = dots(table_low, ups[kk][:rows, order[q]]).astype(jnp.bfloat16)
        x_out[0] = x_s[...]
        up_out[0] = up_s[...]

    def body(parts):
        gates, upw, outs = parts[0::3], parts[1::3], parts[2::3]
        wide = gates[0].shape[1]
        cut = [slice(q * span, (q + 1) * span) for q in range(piece_count)]
        a = sum(dots(x_s[:, cut[q]], gates[q][...]) for q in range(piece_count))
        u = sum(dots(x_s[:, cut[q]], upw[q][...]) for q in range(piece_count))
        back = sum(dots(up_s[:, cut[q]], outs[q][...]) for q in range(piece_count))
        s = 1.0 / (1.0 + jnp.exp(-a))
        silu = a * s
        act = (silu * u).astype(jnp.bfloat16).astype(jnp.float32)
        gg_acc[...] += jnp.sum(act * back, axis=1, keepdims=True)
        gate = gate_s[...]
        act_low = (act * gate).astype(jnp.bfloat16)
        back = back * gate
        gate_grad = (back * u * s * (1.0 + a * (1.0 - s))).astype(jnp.bfloat16)
        up_grad = (back * silu).astype(jnp.bfloat16)
        at = pl.multiple_of(step_f * wide, wide)
        total = gug_out.shape[2] // 2
        gug_out[0, :, pl.ds(at, wide)] = gate_grad
        gug_out[0, :, pl.ds(pl.multiple_of(total + at, wide), wide)] = up_grad
        act_out[0, :, pl.ds(at, wide)] = act_low
        for q in range(piece_count):
            y_acc[:, cut[q]] += dots_nt(act_low, outs[q][...])
            sent_acc[:, cut[q]] += dots_nt(gate_grad, gates[q][...]) + dots_nt(up_grad, upw[q][...])

    @pl.when(step_e == 0)
    def _():
        body(weights[: 3 * piece_count])

    @pl.when(step_e == 1)
    def _():
        body(weights[3 * piece_count :])

    def finish(first):
        which = lax.broadcasted_iota(jnp.int32, (experts, rows), 0) == expert
        for kk, (sent, mix) in enumerate(((sent0, mix0), (sent1, mix1))):
            table = table_s[kk]
            at = slice(kk * half, (kk + 1) * half)
            for q in range(piece_count):
                cols = slice(q * span, (q + 1) * span)
                for out, acc, size in ((sent, sent_acc, rows), (mix, y_acc, rows)):
                    part = lax.dot_general(
                        table, acc[at, cols].astype(jnp.bfloat16), (((0,), (0,)), ((), ())),
                        preferred_element_type=jnp.float32,
                    )
                    if not first:
                        part = part + out[:rows, order[q]].astype(jnp.float32)
                    out[:rows, order[q]] = part.astype(jnp.bfloat16)
            gg = jnp.sum(jnp.where(table > 0, gg_acc[at, :], 0.0), axis=0, keepdims=True)
            gg_rows[kk] += jnp.where(which, gg, 0.0)
            if not first:
                high = gg_rows[kk].astype(jnp.bfloat16)
                sent[rows:, :] = jnp.zeros((sent.shape[0] - rows, sent.shape[1]), jnp.bfloat16)
                sent[rows:, :rows] = high
                sent[rows:, rows : 2 * rows] = (gg_rows[kk] - high.astype(jnp.float32)).astype(jnp.bfloat16)

    last = pl.num_programs(1) - 1

    @pl.when((step_f == last) & (step_e == 0))
    def _():
        finish(True)

    @pl.when((step_f == last) & (step_e == 1))
    def _():
        finish(False)


def run_experts(block, tok, ups, router_t, pieces, capacity, held):
    blocks, _, rows, width = tok.shape
    count, quarter, wide3 = pieces.shape[1:]
    units = wide3 // 3
    tile = min(256, units)
    steps = units // tile
    cap2 = 2 * capacity
    low = jnp.bfloat16
    once = pl.Buffered(1)
    block_of = lambda a, j: pl.BlockSpec(
        (None, None) + a.shape[2:], lambda e, f: (block, j, 0, 0), pipeline_mode=once
    )
    in_specs = [block_of(tok, 0), block_of(tok, 1), block_of(ups, 0), block_of(ups, 1)]
    in_specs.append(pl.BlockSpec(router_t.shape, lambda e, f: (0, 0), pipeline_mode=once))
    operands = [tok, tok, ups, ups, router_t]
    for j in range(2):
        for q in range(count):
            for part in range(3):
                def at(e, f, j=j, q=q, part=part):
                    step = jnp.where(e == 0, f, steps - 1) if j == 0 else jnp.where(e == 1, f, 0)
                    return (j, q, 0, part * steps + step)
                in_specs.append(pl.BlockSpec((None, None, quarter, tile), at))
                operands.append(pieces)
    aliases = {}
    if held is not None:
        for i, a in enumerate(held):
            aliases[len(operands)] = i
            operands.append(a)
            in_specs.append(pl.BlockSpec(memory_space=pl.ANY))
    store = lambda cols: pl.BlockSpec((1, cap2, cols), lambda e, f: (e, block, 0))
    whole_out = lambda r: pl.BlockSpec((r, width), lambda e, f: (0, 0), pipeline_mode=once)
    ext = ups.shape[2]
    struct = jax.ShapeDtypeStruct
    experts = router_t.shape[0]

    def kernel(*refs):
        n_in = 5 + 6 * count
        held_n = 4 if held is not None else 0
        expert_kernel(blocks, capacity, count, *refs[:n_in], *refs[n_in + held_n :])

    return pl.pallas_call(
        kernel,
        grid=(2, steps),
        in_specs=in_specs,
        out_specs=[
            store(width), store(width), store(2 * units), store(units),
            whole_out(ext), whole_out(ext), whole_out(rows), whole_out(rows),
        ],
        out_shape=[
            struct((2, blocks * cap2, width), low), struct((2, blocks * cap2, width), low),
            struct((2, blocks * cap2, 2 * units), low), struct((2, blocks * cap2, units), low),
            struct((ext, width), low), struct((ext, width), low),
            struct((rows, width), low), struct((rows, width), low),
        ],
        scratch_shapes=[
            pltpu.VMEM((cap2, width), low), pltpu.VMEM((cap2, width), low),
            pltpu.VMEM((2, capacity, rows), low), pltpu.VMEM((cap2, 1), jnp.float32),
            pltpu.VMEM((cap2, width), jnp.float32), pltpu.VMEM((cap2, width), jnp.float32),
            pltpu.VMEM((cap2, 1), jnp.float32),
            pltpu.VMEM((experts, rows), jnp.float32), pltpu.VMEM((experts, rows), jnp.float32),
            pltpu.VMEM((2, experts, rows), jnp.float32),
        ],
        input_output_aliases=aliases,
        compiler_params=pltpu.CompilerParams(vmem_limit_bytes=60 * 2**20),
    )(*operands)


low = jnp.bfloat16


def swap_on(value, axis, mask):
    count = lax.axis_size(axis)
    return lax.ppermute(value, axis, [(i, i ^ mask) for i in range(count)])


def after(value, *others):
    return lax.optimization_barrier((value, *others))[0]


def line_chain(block, axis, then=None):
    n = lax.axis_size(axis)
    rights, lefts = [block], [block]
    for s in range(1, n):
        if s == 2 and then is not None:
            rights[1], lefts[1] = after(rights[1], then), after(lefts[1], then)
        rights.append(lax.ppermute(rights[-1], axis, [(i, i + 1) for i in range(s - 1, n - 1)]))
        lefts.append(lax.ppermute(lefts[-1], axis, [(i, i - 1) for i in range(1, n - s + 1)]))
    return rights, lefts


def shift_back(value, axis, s):
    n = lax.axis_size(axis)
    return lax.ppermute(value, axis, [(i, (i - s) % n) for i in range(n)])


def sum_all(value):
    for axis in ("grp", "ctx", "exp"):
        mask = 1
        while mask < lax.axis_size(axis):
            value = value + swap_on(value, axis, mask)
            mask *= 2
    return value


def add_low(a, b):
    return (a.astype(jnp.float32) + b.astype(jnp.float32)).astype(low)


def pick(array, index):
    return lax.dynamic_index_in_dim(array, index, 0, keepdims=False)


def per_device(
    hidden_in,
    out_grad,
    doc_lengths,
    routes,
    attention_input_weight,
    attn_out_weight,
    norm_gains,
    head_gains,
    router_weight,
    expert_in,
    expert_out,
):
    hidden = hidden_in[0].astype(jnp.float32)
    rows, width = hidden.shape
    head_dim = head_gains.shape[0]
    expert_count = router_weight.shape[1]
    top = routes.shape[2]
    n_ctx, n_exp = lax.axis_size("ctx"), lax.axis_size("exp")
    grp, ctx, exp = lax.axis_index("grp"), lax.axis_index("ctx"), lax.axis_index("exp")
    half, core = ctx // 2, ctx % 2
    length = rows * n_ctx
    query_width = attn_out_weight.shape[1]
    kv_width = (attention_input_weight.shape[1] - query_width) // 2
    heads = query_width // head_dim // n_ctx
    shard = attention_input_weight.shape[0]
    f32 = jnp.float32

    def dot(a, b):
        return jnp.dot(a, b, preferred_element_type=f32)

    def dot_nt(a, b):
        return lax.dot_general(a, b, (((1,), (1,)), ((), ())), preferred_element_type=f32)

    def dot_tn(a, b):
        return lax.dot_general(a, b, (((0,), (0,)), ((), ())), preferred_element_type=f32)

    def by_exp(a):
        return a.reshape(a.shape[0], n_ctx, n_exp, shard).transpose(0, 2, 1, 3).reshape(a.shape)

    def by_ctx(a):
        return a.reshape(a.shape[0], n_exp, n_ctx, shard).transpose(0, 2, 1, 3).reshape(a.shape)

    def own_half_first(a):
        return jnp.where(half == 0, a, jnp.concatenate([a[:, width // 2 :], a[:, : width // 2]], 1))

    def gather_ctx(block):
        over = swap_on(block, "ctx", 2)
        blocks = [block, swap_on(block, "ctx", 1), over, swap_on(over, "ctx", 1)]
        return place_ctx(blocks)

    def place_ctx(blocks):
        out = jnp.zeros((n_ctx,) + blocks[0].shape, blocks[0].dtype)
        for m in range(n_ctx):
            out = lax.dynamic_update_index_in_dim(out, blocks[m], ctx ^ m, 0)
        return out

    def scatter_ctx(parts):
        got = swap_on(jnp.stack([pick(parts, ctx ^ 1), pick(parts, ctx ^ 3)]), "ctx", 1)
        mine = pick(parts, ctx).astype(f32) + got[0].astype(f32)
        other = add_low(pick(parts, ctx ^ 2), got[1])
        return mine + swap_on(other, "ctx", 2).astype(f32)

    positions = jnp.arange(length, dtype=jnp.int32)
    relative = doc_tables(doc_lengths[0], positions)[1]
    doc_start = (positions - relative)[None, :]
    freqs = rotary_base ** (-2.0 * jnp.arange(head_dim // 2, dtype=f32) / head_dim)
    angles = relative.astype(f32)[:, None] * freqs[None, :]
    cosine = jnp.concatenate([jnp.cos(angles)] * 2, 1)
    sine = jnp.concatenate([-jnp.sin(angles), jnp.sin(angles)], 1)
    gains = jnp.pad(head_gains.astype(f32).T, ((0, 6), (0, 0)))
    gain_attn = norm_gains[:, 0].astype(f32)
    gain_ffn = norm_gains[:, 1].astype(f32)

    by_head = lambda a, at, size: a[:, at : at + n_ctx * size].reshape(shard, n_ctx, size).transpose(1, 0, 2)
    wide = heads * head_dim
    weight_in_block = jnp.concatenate(
        [
            by_head(attention_input_weight, 0, wide),
            by_head(attention_input_weight, query_width, head_dim),
            by_head(attention_input_weight, query_width + kv_width, head_dim),
        ],
        2,
    ).reshape(n_ctx * shard, wide + 2 * head_dim)
    weight_out_block = by_head(attn_out_weight, 0, wide).reshape(n_ctx * shard, wide)

    normed, hidden_unit, hidden_scale = norm_forward(hidden, gain_attn)
    capacity = 5 * rows * top // (4 * expert_count)
    hits = jnp.any(routes[0][:, :, None] == jnp.arange(expert_count, dtype=jnp.int32), axis=1)
    before = jnp.tril(jnp.ones((rows, rows), low), -1)
    slots = jnp.where(hits, dot(before, hits.astype(low)), -1.0).T.astype(low)
    upstream_block = jnp.concatenate(
        [own_half_first(out_grad[0]), jnp.pad(slots, ((0, 0), (0, width - rows)))]
    )
    local_experts, quarter, hidden_units = expert_in.shape[1], expert_in.shape[0], expert_out.shape[2]
    expert_rows = jnp.concatenate(
        [expert_in.transpose(1, 0, 2, 3).reshape(local_experts, quarter, -1), expert_out.transpose(1, 0, 2)], 2
    )
    (
        weight_in, weight_out, normed_seq, qkv, attended, expert_weights, upstreams, tokens, log_mass, middle,
    ) = front(
        weight_in_block, weight_out_block, by_exp(normed.astype(low)), expert_rows, upstream_block,
        by_exp(hidden_in[0]), by_exp(gain_ffn[None]), cosine, sine, doc_start, gains, heads, n_ctx, n_exp,
    )
    middle = by_ctx(middle)
    ffn_normed, middle_unit, middle_scale = norm_forward(middle, gain_ffn)
    ffn_low = ffn_normed.astype(low)

    logits = dot(ffn_low, router_weight)
    probs = jax.nn.softmax(logits, axis=-1)
    selected = jnp.where(hits, probs, 0.0)
    sel_total = jnp.sum(selected, axis=-1, keepdims=True)
    gates = selected / sel_total

    router_here = own_half_first(router_weight.T)
    held, backs, mixes = None, [], []
    for s in range(n_exp):
        *held, back0, back1, mix0, mix1 = run_experts(
            s, tokens, upstreams, router_here, expert_weights, capacity, held
        )
        back = add_low(back0, swap_on(back1, "ctx", 1))
        backs.append(back if s == 0 else shift_back(back, "exp", s))
        mixes.append((mix0, mix1))
    back_total = sum(b.astype(f32) for b in backs)
    sent_grads = own_half_first(back_total[:rows])
    gate_grads = (back_total[rows:, :rows] + back_total[rows:, rows : 2 * rows]).T

    inputs_all, ups_all, gate_up_all, act_all = held
    grad_halves = []
    for j in range(2):
        grad = jnp.concatenate(
            [dot_tn(inputs_all[j], gate_up_all[j]), dot_tn(ups_all[j], act_all[j])], 1
        ).astype(low)
        grad_halves.append(
            grad[: width // 2].astype(f32) + swap_on(grad[width // 2 :], "ctx", 2).astype(f32)
        )

    weighted = jnp.sum(gate_grads * gates, axis=1, keepdims=True)
    prob_grads = jnp.where(hits, (gate_grads - weighted) / sel_total, 0.0)
    logit_grads = probs * (prob_grads - jnp.sum(probs * prob_grads, axis=1, keepdims=True))
    router_float = router_weight.astype(f32)
    ffn_grads = sent_grads + jnp.dot(logit_grads, router_float.T, precision=lax.Precision.HIGHEST)
    router_grads = jnp.dot(ffn_low.astype(f32).T, logit_grads, precision=lax.Precision.HIGHEST)
    middle_grad = out_grad[0].astype(f32) + norm_backward(ffn_grads, middle_unit, middle_scale, gain_ffn)

    branch_grad = gather_ctx(by_exp(middle_grad.astype(low))).reshape(length, width)
    heads_grad = dot(branch_grad, weight_out).astype(low)
    joined_grads, gain_grads = attend_back(
        qkv, cosine, sine, doc_start, gains, attended, heads_grad, log_mass, heads
    )
    part_out = dot_tn(branch_grad, attended).astype(low)
    part_in = dot_tn(normed_seq, joined_grads).astype(low)
    normed_parts = dot_nt(joined_grads, weight_in).astype(low).reshape(n_ctx, rows, width)
    normed_grads = by_ctx(scatter_ctx(normed_parts))
    input_part = norm_backward(normed_grads, hidden_unit, hidden_scale, gain_attn)
    input_grad = (middle_grad + input_part).astype(low)[None]

    mixture = 0.0
    for s, (own, other) in enumerate(mixes):
        mix = add_low(own, swap_on(after(other, back_total), "ctx", 1))
        mixture = mixture + (mix if s == 0 else shift_back(mix, "exp", s)).astype(f32)
    mixture = own_half_first(mixture)
    output = (middle + mixture).astype(low)[None]

    kept = add_low(grad_halves[1], swap_on(grad_halves[0].astype(low), "grp", 1)).reshape(2, quarter, -1)
    mine, sibling = kept[0], swap_on(kept[1], "ctx", 1)
    mine_x, sibling_x = swap_on(mine, "grp", 1), swap_on(sibling, "grp", 1)
    totals = []
    for at in range(local_experts):
        same_core = at // 2 == core
        same_grp = at % 2 == grp
        totals.append(
            jnp.where(
                same_core, jnp.where(same_grp, mine, mine_x), jnp.where(same_grp, sibling, sibling_x)
            ).astype(f32)
        )
    total = jnp.stack(totals, 1)
    expert_in_grad = total[:, :, : 2 * hidden_units].reshape(expert_in.shape)
    expert_out_grad = total[:, :, 2 * hidden_units :]

    def to_rows(part):
        blocks = part.reshape(n_exp, n_ctx * shard, part.shape[1])
        own = pick(blocks, exp).astype(f32)
        for s in range(1, n_exp):
            own = own + shift_back(pick(blocks, (exp - s) % n_exp), "exp", s).astype(f32)
        own = own.astype(low).reshape(n_ctx, shard, part.shape[1])
        pieces = [pick(own, ctx)] + [swap_on(pick(own, ctx ^ m), "ctx", m) for m in range(1, n_ctx)]
        placed = place_ctx(pieces)
        return placed.astype(f32) + swap_on(placed, "grp", 1).astype(f32)

    rows_out = to_rows(part_out)
    rows_in = to_rows(part_in)
    attn_out_grad = rows_out.transpose(1, 0, 2).reshape(shard, query_width)
    attn_in_grad = jnp.concatenate(
        [
            rows_in[:, :, :wide].transpose(1, 0, 2).reshape(shard, query_width),
            rows_in[:, :, wide : wide + head_dim].transpose(1, 0, 2).reshape(shard, kv_width),
            rows_in[:, :, wide + head_dim :].transpose(1, 0, 2).reshape(shard, kv_width),
        ],
        1,
    )

    norm_gain_grads = jnp.stack(
        [jnp.sum(normed_grads * hidden_unit, axis=0), jnp.sum(ffn_grads * middle_unit, axis=0)], axis=1
    )
    small = [norm_gain_grads, gain_grads[:2].T, router_grads]
    summed = sum_all(jnp.concatenate([a.reshape(-1, head_dim) for a in small]))
    norm_total, head_total, router_total = (
        part.reshape(a.shape)
        for a, part in zip(
            small, jnp.split(summed, [norm_gain_grads.size // head_dim, norm_gain_grads.size // head_dim + 2])
        )
    )
    return (
        output,
        input_grad,
        attn_in_grad,
        attn_out_grad,
        norm_total,
        head_total,
        router_total,
        expert_in_grad,
        expert_out_grad,
    )


def solution(mesh):
    placed = (
        P(("grp", "exp"), "ctx", None),
        P(("grp", "exp"), "ctx", None),
        P(("grp", "exp"), None),
        P(("grp", "exp"), "ctx", None),
        P(("ctx", "exp"), None),
        P(("ctx", "exp"), None),
        P(),
        P(),
        P(),
        P("ctx", "exp", None, None),
        P("ctx", "exp", None),
    )
    sizes = dict(mesh.shape)
    body = per_device if sizes == {"grp": 2, "ctx": 4, "exp": 4} else per_device_general
    return jax.shard_map(
        body,
        mesh=mesh,
        in_specs=placed,
        out_specs=(
            P(("grp", "exp"), "ctx", None),
            P(("grp", "exp"), "ctx", None),
            P(("ctx", "exp"), None),
            P(("ctx", "exp"), None),
            P(),
            P(),
            P(),
            P("ctx", "exp", None, None),
            P("ctx", "exp", None),
        ),
        check_vma=False,
    )
```
